512 devices in a mesh: rad: 32 (over z_hi, x, core), lat: 16 (over z_lo, y).
Axes of the slice: x: 4, y: 8, z: 8 (z_hi: 4, z_lo: 2; z = z_hi * 2 + z_lo), core: 2. Of those that a mesh axis runs over, the one named last changes fastest.
Arguments:
- nonlinear_samples: bfloat16 [32, 2, 1536, 3072], P('rad', None, 'lat'), may hold values from -6 to 6
- legendre: bfloat16 [256, 1536, 1024], P('rad', 'lat'), may hold values from -0.21875 to 0.21875
- assign: int32 [256], replicated, may hold values from 0 to 255, each once
- counts: int32 [256], replicated, may hold values from 513 to 1024, as said below
- spectral_state: float32 [1024, 256, 128], P('lat', 'rad'), may hold values from -6 to 6
- inverses: float32 [1024, 4, 8, 8], P('lat'), may hold values from -1 to 1
Outputs:
- advanced: float32 [1024, 256, 128], P('lat', 'rad')
The draws below stay inside these ranges and needn't reach their ends.
Inputs may be any that keep to these rules, and one draw needn't show every extreme that they name: Slot s carries order assign[s]; each order 0 to 255 stands in exactly one slot. counts[m] is at most 1024 - m, and order 0 has 1024 live degrees.
All inputs are finite; a program needn't handle non-finite values.
Results may differ from the reference program's by a relative error of at most 0.0034.
Values may be sent and summed in bfloat16 or wider, within the bound.
A program may use at most 64 MiB of HBM per device.

```python
import math
import jax
import jax.numpy as jnp
from jax import lax

NPHI = 3072
NLAT = 1536
LMAX = 1024
KB = 8
NR = 32
ORD = 256
NB = 4
LAT_DEV = 96


def draw_counts(key, part):
    orders = jnp.arange(ORD, dtype=jnp.int32)
    dropped = jax.random.randint(jax.random.fold_in(key, 11), (ORD,), 0, LMAX // 4 + 1, dtype=jnp.int32)
    values = LMAX - orders - dropped
    return jnp.where(orders == 0, LMAX, values).astype(jnp.int32)


def draw_inverses(key, part):
    radial_spacing = 0.65 / (NR + 1)
    block_ids = jnp.arange(NB, dtype=jnp.float32)
    middle = 0.35 + 0.65 * ((block_ids + 0.5) * KB + 0.5) / (NR + 1)
    degree = jnp.arange(LMAX, dtype=jnp.float32)
    scales = 1.0 / (2.0 + 0.5 * radial_spacing * radial_spacing * degree[:, None] * (degree[:, None] + 1.0) / (middle[None, :] * middle[None, :]))
    random_noise_key = jax.random.fold_in(key, 21)
    diag_key = jax.random.fold_in(key, 22)
    noise = 0.45 * jnp.clip(jax.random.normal(random_noise_key, (LMAX, NB, KB, KB), jnp.float32), -3.0, 3.0)
    noise = noise / math.sqrt(KB)
    diagonal = 1.0 + 0.5 * jax.random.uniform(diag_key, (LMAX, NB, 1, KB), jnp.float32)
    identity = jnp.eye(KB, dtype=jnp.float32)
    return (scales[:, :, None, None] * (identity * diagonal + noise)).astype(jnp.float32)


def strengthened(array, stream_key, source, target, blocks, factor):
    owner, partner = [(jnp.arange(array.shape[dim]) // (array.shape[dim] // blocks)).reshape([-1 if axis == dim else 1 for axis in range(array.ndim)]) for dim in (source, target)]
    chosen = jax.random.permutation(stream_key, blocks)[partner]
    strong = (owner == chosen) | (owner == (partner + blocks // 2) % blocks)
    return jnp.where(strong, factor * array, array)


def block_scale(own_key, dims, shards, low, top_value):
    loudness, own = 1.0, jax.random.fold_in(own_key, 6)
    for dim, parts in shards:
        heights = jnp.exp(jax.random.uniform(jax.random.fold_in(own, dim), (parts,), jnp.float32, low / len(shards), top_value / len(shards)))
        loudness = loudness * jnp.repeat(heights, dims[dim] // parts).reshape([-1 if axis == dim else 1 for axis in range(len(dims))])
    return loudness


def normal_values(rng, extent, spread, bound, shards=(), kind=jnp.bfloat16):
    array = spread * jax.random.normal(rng, extent, jnp.float32)
    if shards:
        array = array * block_scale(rng, extent, shards, -0.22, 0.18)
    return jnp.clip(array, -bound, bound).astype(kind)


def noise_with(key, extent, scale, reach, split, heavy, held_as=jnp.bfloat16):
    values = scale * jax.random.normal(key, extent, jnp.float32)
    if split:
        values = values * block_scale(key, extent, split, -0.22, 0.18)
    return jnp.clip(strengthened(values, jax.random.fold_in(key, 3), *heavy), -reach, reach).astype(held_as)


def setup_inputs(seed: int = 0) -> dict:
    streams_of = jax.random.split(jax.random.key(seed), 7)
    nonlinear_samples = normal_values(streams_of[0], (NR, 2, NLAT, NPHI), 1.0, 6.0, ((0, 32), (2, 16)))
    legendre = noise_with(streams_of[1], (ORD, NLAT, LMAX), NLAT ** -0.5, 0.21875, ((0, 32), (1, 16)), (1, 2, 16, 2.0))
    assign = jax.random.permutation(streams_of[2], ORD).astype(jnp.int32)
    counts = draw_counts(jax.random.fold_in(streams_of[6], 71), 0)
    spectral_state = normal_values(streams_of[4], (LMAX, ORD, 4 * NR), 1.0, 6.0, ((0, 16), (1, 32)), jnp.float32)
    inverses = draw_inverses(jax.random.fold_in(streams_of[6], 71), 0)
    return {"nonlinear_samples": nonlinear_samples, "legendre": legendre, "assign": assign, "counts": counts, "spectral_state": spectral_state, "inverses": inverses}


def trig_table(assign, lon_count):
    longitude = jnp.arange(lon_count, dtype=jnp.int32)
    phases = longitude[:, None] * assign[None, :] % lon_count
    angles = phases.astype(jnp.float32) * (2.0 * math.pi / lon_count)
    normalizing_multiplier = 1.0 / math.sqrt(lon_count)
    cosine = (jnp.cos(angles) * normalizing_multiplier).astype(jnp.bfloat16)
    sine = (-jnp.sin(angles) * normalizing_multiplier).astype(jnp.bfloat16)
    return jnp.stack([cosine, sine], axis=2).reshape(lon_count, 2 * assign.shape[0])

def radial_step(spectral_state, source, inverses, degree):
    deg_rows, slot_count, width = spectral_state.shape
    shell_number = width // 4
    blk_size = inverses.shape[2]
    blk_count = shell_number // blk_size
    field_now = spectral_state.reshape(deg_rows, slot_count, 4, shell_number)
    zero_rim = jnp.zeros((deg_rows, slot_count, 4, 1), jnp.float32)
    outward = jnp.concatenate([field_now[..., 1:], zero_rim], axis=3)
    inward = jnp.concatenate([zero_rim, field_now[..., :-1]], axis=3)
    radial_spacing = 0.65 / (shell_number + 1)
    radius = 0.35 + 0.65 * (jnp.arange(shell_number, dtype=jnp.float32) + 1.0) / (shell_number + 1)
    ratios = radial_spacing / radius
    degree_term = degree[:, None, None, None] * (degree[:, None, None, None] + 1.0)
    central = 0.5 * radial_spacing * radial_spacing * degree_term / (radius * radius)
    right_side = field_now + 0.5 * (outward - 2.0 * field_now + inward) + 0.5 * ratios * (outward - inward)
    right_side = right_side - central * field_now + source.reshape(deg_rows, slot_count, 4, shell_number)
    lower_link = -0.5 * (1.0 - ratios[0::blk_size])
    upper_link = -0.5 * (1.0 + ratios[blk_size - 1::blk_size])
    blocks = jnp.moveaxis(right_side.reshape(deg_rows, slot_count, 4, blk_count, blk_size), 3, 0)
    block_inverse = jnp.moveaxis(inverses, 1, 0)
    first_unit = (jnp.arange(blk_size, dtype=jnp.int32) == 0).astype(jnp.float32)
    start_carry = jnp.zeros((deg_rows, slot_count, 4), jnp.float32)

    def forward(carried, items):
        matrix, block, link = items
        block = block - link * carried[..., None] * first_unit
        result = jnp.einsum('lij,locj->loci', matrix, block, precision=lax.Precision.HIGHEST)
        return (result[..., blk_size - 1], result)

    def inverse_sweep(carried, items):
        matrix, partial_solution, link = items
        result = partial_solution - link * carried[..., None] * matrix[:, None, None, :, blk_size - 1]
        return (result[..., 0], result)
    _, forward_blocks = lax.scan(forward, start_carry, (block_inverse, blocks, lower_link))
    _, solved = lax.scan(inverse_sweep, start_carry, (block_inverse, forward_blocks, upper_link), reverse=True)
    return jnp.moveaxis(solved, 0, 3).reshape(deg_rows, slot_count, 4 * shell_number)

def reference(nonlinear_samples, legendre, assign, counts, spectral_state, inverses):
    table = trig_table(assign, NPHI)

    def transform(sheet):
        flat_rows = sheet.reshape(2 * NLAT, NPHI)
        result = jnp.dot(flat_rows, table, preferred_element_type=jnp.float32)
        return result.astype(jnp.bfloat16).reshape(2, NLAT, ORD, 2)
    fourier_modes = lax.map(transform, nonlinear_samples)
    by_slot = jnp.moveaxis(fourier_modes, 3, 0)
    band_total = NLAT // LAT_DEV

    def analyse(items):
        table_slot, values = items
        legendre_table_bands = table_slot.reshape(band_total, LAT_DEV, LMAX).astype(jnp.float32)
        value_bands = values.reshape(NR, 2, band_total, LAT_DEV, 2).astype(jnp.float32)
        partial_value = jnp.einsum('btl,rfbtk->blfkr', legendre_table_bands, value_bands)
        partial_value = lax.optimization_barrier(partial_value.astype(jnp.bfloat16)).astype(jnp.float32)
        return lax.optimization_barrier(jnp.sum(partial_value, axis=0)).reshape(LMAX, 4 * NR)
    summed = lax.map(analyse, (legendre, by_slot))
    summed = jnp.moveaxis(summed, 0, 1)
    degree_ids = jnp.arange(LMAX, dtype=jnp.int32)
    limits = assign + counts[assign]
    live = (degree_ids[:, None] >= assign[None, :]) & (degree_ids[:, None] < limits[None, :])
    source = jnp.where(live[:, :, None], summed, jnp.zeros_like(summed))
    return radial_step(spectral_state, source, inverses, degree_ids.astype(jnp.float32))
```

```python
import functools
import math

import jax
import jax.numpy as jnp
from jax import lax
from jax.experimental import pallas as pl
from jax.experimental.pallas import tpu as pltpu
from jax.sharding import PartitionSpec as P

MESH = pl.DeviceIdType.MESH
F32 = jnp.float32
BF16 = jnp.bfloat16
FAR = ((0, 1), (2, 3))


def kernel(
    n_rad,
    samples,
    legendre,
    cos_a,
    sin_a,
    cos_b,
    sin_b,
    state,
    inverses,
    live,
    out,
    table,
    send_rows,
    got_rows,
    rows32,
    modes,
    leg_own,
    leg_got,
    leg_mat,
    send_buf,
    recv_buf,
    acc,
    fields,
    right,
    solved,
    own_sem,
    zs_sem,
    zr_sem,
    as_sem,
    ar_sem,
    rs_sem,
    rr_sem,
):
    rad = lax.axis_index("rad")
    lat = lax.axis_index("lat")
    z = lat // 8
    y = lat % 8
    other = (1 - z) * 8 + y
    y_next = (z * 8 + (y + 1) % 8, z * 8 + (y + 7) % 8)
    n_r = n_rad
    kb = n_r // 4
    comps = 4 * n_r
    lon_a = cos_a.shape[0]
    lon_b = cos_b.shape[0]
    slots = cos_a.shape[1]

    barrier = pltpu.get_barrier_semaphore()

    @pl.loop(1, n_rad)
    def _(i):
        peer = (rad + i) % n_rad
        pl.semaphore_signal(barrier, inc=1, device_id=(peer, lat), device_id_type=MESH)
        pl.semaphore_signal(barrier, inc=1, device_id=(peer, other), device_id_type=MESH)

    pl.semaphore_signal(barrier, inc=1, device_id=(rad, other), device_id_type=MESH)
    for d in range(2):
        pl.semaphore_signal(barrier, inc=1, device_id=(rad, y_next[d]), device_id_type=MESH)

    tile_of = [(y // 2 + o) % 4 for o in (2, 1, 3, 0)]

    def own_copy(c):
        lanes = pl.multiple_of(z * 512 + tile_of[c] * 128, 128)
        return pltpu.make_async_copy(
            legendre.at[:, :, pl.ds(lanes, 128)], leg_own.at[tile_of[c]], own_sem.at[c]
        )

    def z_copy(c):
        lanes = pl.multiple_of((1 - z) * 512 + tile_of[c] * 128, 128)
        return pltpu.make_async_remote_copy(
            src_ref=legendre.at[:, :, pl.ds(lanes, 128)],
            dst_ref=leg_got.at[tile_of[c]],
            send_sem=zs_sem.at[c],
            recv_sem=zr_sem.at[c],
            device_id=(rad, other),
            device_id_type=MESH,
        )

    for c in range(4):
        own_copy(c).start()

    @pl.loop(0, lon_a)
    def _(a):
        ca = cos_a[pl.ds(a, 1), :]
        sa = sin_a[pl.ds(a, 1), :]
        cb = cos_b[...]
        sb = sin_b[...]
        at = pl.multiple_of(a * lon_b, lon_b)
        table[pl.ds(at, lon_b), 0:slots] = (ca * cb - sa * sb).astype(BF16)
        table[pl.ds(at, lon_b), slots : 2 * slots] = (-(sa * cb + ca * sb)).astype(BF16)

    pl.semaphore_wait(barrier, 2 * (n_rad - 1) + 3)
    for c in range(4):
        z_copy(c).start()

    fourier = jnp.dot(samples[...], table[...], preferred_element_type=F32)
    fourier = fourier.astype(BF16).astype(F32)
    for f in range(2):
        part = fourier[96 * f : 96 * (f + 1)]
        part = jnp.concatenate([part, jnp.zeros((32, 2 * slots), F32)], axis=0)
        flipped = part.T
        both = jnp.concatenate(
            [
                flipped[:slots].reshape(n_rad, 8, 128),
                flipped[slots:].reshape(n_rad, 8, 128),
            ],
            axis=1,
        )
        send_rows[:, 16 * f : 16 * (f + 1), :] = both.astype(BF16)

    def a2a(peer, other_side):
        return pltpu.make_async_remote_copy(
            src_ref=send_rows.at[peer],
            dst_ref=got_rows.at[z, rad],
            send_sem=as_sem.at[other_side],
            recv_sem=ar_sem.at[other_side],
            device_id=(peer, other if other_side else lat),
            device_id_type=MESH,
        )

    a2a(rad, 1).start()

    @pl.loop(1, n_rad)
    def _(i):
        peer = (rad + i) % n_rad
        a2a(peer, 0).start()
        a2a(peer, 1).start()

    got_rows[z, rad] = send_rows[rad]

    leg_mat[:, :, :, 96:128, :] = jnp.zeros((2, 8, 4, 32, 128), BF16)
    leg_mat[:, :, :, 224:256, :] = jnp.zeros((2, 8, 4, 32, 128), BF16)
    low = lax.broadcasted_iota(jnp.int32, (96, 128), 1) < 64

    def lay(source, band, tile):
        @pl.loop(0, 4)
        def _(p):
            a = source[tile, 2 * p].astype(F32)
            b = source[tile, 2 * p + 1].astype(F32)
            ra = pltpu.roll(a, 64, 1)
            rb = pltpu.roll(b, 64, 1)
            zero = jnp.zeros_like(a)
            leg_mat[band, 2 * tile, p, 0:96, :] = jnp.where(low, a, zero).astype(BF16)
            leg_mat[band, 2 * tile, p, 128:224, :] = jnp.where(low, zero, rb).astype(BF16)
            leg_mat[band, 2 * tile + 1, p, 0:96, :] = jnp.where(low, ra, zero).astype(BF16)
            leg_mat[band, 2 * tile + 1, p, 128:224, :] = jnp.where(low, zero, b).astype(BF16)

    for c in range(4):
        own_copy(c).wait()
        lay(leg_own, 0, tile_of[c])

    for p in range(4):
        pair = jnp.concatenate(
            [state[pl.ds(2 * p, 64, stride=8), :], state[pl.ds(2 * p + 1, 64, stride=8), :]], axis=0
        )
        fields[comps * p : comps * (p + 1), :] = pair.T

    spacing = 0.65 / (n_r + 1)
    radius = [0.35 + 0.65 * (i + 1.0) / (n_r + 1) for i in range(n_r)]
    degree = (lat * 64 + lax.broadcasted_iota(jnp.int32, (1, 128), 1) % 64).astype(F32)
    square = 0.5 * spacing * spacing * degree * (degree + 1.0)
    for i in range(n_r):
        now = fields[pl.ds(i, 16, stride=n_r), :]
        value = -(square * (1.0 / (radius[i] * radius[i]))) * now
        ratio = spacing / radius[i]
        if i + 1 < n_r:
            value = value + (0.5 + 0.5 * ratio) * fields[pl.ds(i + 1, 16, stride=n_r), :]
        if i > 0:
            value = value + (0.5 - 0.5 * ratio) * fields[pl.ds(i - 1, 16, stride=n_r), :]
        right[pl.ds(i, 16, stride=n_r), :] = value

    def regroup(band, side):
        rows32[...] = got_rows[band].reshape(n_rad * 32, 128).astype(F32)
        for s in range(8):
            for c in range(4):
                modes[side, s // 2, n_r * c : n_r * (c + 1), 128 * (s % 2) : 128 * (s % 2 + 1)] = (
                    rows32[pl.ds(8 * c + s, n_r, stride=32), :].astype(BF16)
                )

    def arrival(side, first):
        band = z if side == 0 else 1 - z
        return pltpu.make_async_remote_copy(
            src_ref=send_rows.at[pl.ds(first, n_rad - first)],
            dst_ref=got_rows.at[band, pl.ds(first, n_rad - first)],
            send_sem=as_sem.at[side],
            recv_sem=ar_sem.at[side],
            device_id=(rad, other),
            device_id_type=MESH,
        )

    arrival(0, 1).wait_recv()
    regroup(z, 0)
    arrival(1, 0).wait_recv()
    regroup(1 - z, 1)

    def own(d, p):
        total = None
        for side in range(2):
            band = jnp.dot(modes[side, p], leg_mat[side, d, p], preferred_element_type=F32)
            band = band.astype(BF16).astype(F32)
            total = band if total is None else total + band
        return total

    def hop(way, h, p):
        i = (way * 4 + h - 1) * 4 + p
        return pltpu.make_async_remote_copy(
            src_ref=send_buf.at[way, h - 1, p],
            dst_ref=recv_buf.at[way, h - 1, p],
            send_sem=rs_sem.at[i],
            recv_sem=rr_sem.at[i],
            device_id=(rad, y_next[way]),
            device_id_type=MESH,
        )

    for h in (4, 3, 2, 1):
        for c in {4: (0,), 3: (1, 2), 2: (), 1: (3,)}[h]:
            z_copy(c).wait_recv()
            lay(leg_got, 1, tile_of[c])
        for p in range(4):
            for way in range(2):
                if h == 4 and p not in FAR[way]:
                    continue
                d = (y + h) % 8 if way == 0 else (y + 8 - h) % 8
                total = own(d, p)
                if h < 3 or (h == 3 and p in FAR[way]):
                    hop(way, h + 1, p).wait_recv()
                    total = total + recv_buf[way, h, p]
                send_buf[way, h - 1, p] = total
                hop(way, h, p).start()

    for p in range(4):
        acc[comps * p : comps * (p + 1), :] = own(y, p)
    for p in range(4):
        total = acc[comps * p : comps * (p + 1), :]
        for way in range(2):
            hop(way, 1, p).wait_recv()
            total = total + recv_buf[way, 0, p]
        total = jnp.where(live[p : p + 1, :] > 0, total, jnp.zeros_like(total))
        rows = slice(comps * p, comps * (p + 1))
        right[rows, :] = right[rows, :] + total

    ratios = [spacing / radius[i] for i in range(n_r)]
    lower = [-0.5 * (1.0 - ratios[k * kb]) for k in range(4)]
    upper = [-0.5 * (1.0 + ratios[(k + 1) * kb - 1]) for k in range(4)]
    carried = None
    forward = []
    for k in range(4):
        b = [right[pl.ds(k * kb + j, 16, stride=n_r), :] for j in range(kb)]
        if k > 0:
            b[0] = b[0] - lower[k] * carried
        rows = []
        for i in range(kb):
            value = None
            for j in range(kb):
                at = (k * kb + i) * kb + j
                term = inverses[at : at + 1, :] * b[j]
                value = term if value is None else value + term
            rows.append(value)
        forward.append(rows)
        carried = rows[kb - 1]
    carried = None
    for k in (3, 2, 1, 0):
        rows = forward[k]
        if k < 3:
            scaled = upper[k] * carried
            rows = [
                rows[i]
                - scaled * inverses[(k * kb + i) * kb + kb - 1 : (k * kb + i) * kb + kb, :]
                for i in range(kb)
            ]
        carried = rows[0]
        for i in range(kb):
            solved[pl.ds(k * kb + i, 16, stride=n_r), :] = rows[i]
    for p in range(4):
        flipped = solved[comps * p : comps * (p + 1), :].T
        out[pl.ds(2 * p, 64, stride=8), :] = flipped[:64]
        out[pl.ds(2 * p + 1, 64, stride=8), :] = flipped[64:]

    for c in range(4):
        z_copy(c).wait_send()
    arrival(0, 1).wait_send()
    arrival(1, 0).wait_send()
    for h in (4, 3, 2, 1):
        for p in range(4):
            for way in range(2):
                if h < 4 or p in FAR[way]:
                    hop(way, h, p).wait_send()


def body(n_rad, samples, legendre, assign, counts, spectral_state, inverses):
    lon = samples.shape[3]
    lon_b = 32
    lon_a = lon // lon_b
    rad = lax.axis_index("rad")
    lat = lax.axis_index("lat")
    kb = inverses.shape[2]
    n_r = 4 * kb
    comps = 4 * n_r
    order = assign[None, :]
    phase_a = jnp.arange(lon_a, dtype=jnp.int32)[:, None] * order % lon_a
    phase_b = jnp.arange(lon_b, dtype=jnp.int32)[:, None] * order % lon
    angle_a = phase_a.astype(F32) * (2.0 * math.pi / lon_a)
    angle_b = phase_b.astype(F32) * (2.0 * math.pi / lon)
    unit = 1.0 / math.sqrt(lon)
    cos_a, sin_a = jnp.cos(angle_a), jnp.sin(angle_a)
    cos_b, sin_b = jnp.cos(angle_b) * unit, jnp.sin(angle_b) * unit

    mine = lax.dynamic_slice_in_dim(assign, rad * 8, 8, 0)
    ids = jnp.arange(counts.shape[0], dtype=jnp.int32)
    held = jnp.sum(jnp.where(mine[:, None] == ids[None, :], counts[None, :], 0), axis=1)
    degrees = lat * 64 + jnp.arange(64, dtype=jnp.int32)
    live = (degrees[None, :] >= mine[:, None]) & (degrees[None, :] < (mine + held)[:, None])
    live = live.astype(F32).reshape(4, 128)

    inv = jnp.transpose(inverses, (1, 2, 3, 0)).reshape(4 * kb * kb, 64)
    inv = jnp.concatenate([inv, inv], axis=1)

    vmem = pl.BlockSpec(memory_space=pltpu.VMEM)
    out = pl.pallas_call(
        functools.partial(kernel, n_rad),
        out_shape=jax.ShapeDtypeStruct((512, comps), F32),
        in_specs=[vmem, pl.BlockSpec(memory_space=pl.ANY)] + [vmem] * 7,
        out_specs=vmem,
        scratch_shapes=[
            pltpu.VMEM((lon, 2 * assign.shape[0]), BF16),
            pltpu.VMEM((n_rad, 32, 128), BF16),
            pltpu.VMEM((2, n_rad, 32, 128), BF16),
            pltpu.VMEM((n_rad * 32, 128), F32),
            pltpu.VMEM((2, 4, comps, 256), BF16),
            pltpu.VMEM((4, 8, 96, 128), BF16),
            pltpu.VMEM((4, 8, 96, 128), BF16),
            pltpu.VMEM((2, 8, 4, 256, 128), BF16),
            pltpu.VMEM((2, 4, 4, comps, 128), F32),
            pltpu.VMEM((2, 4, 4, comps, 128), F32),
            pltpu.VMEM((4 * comps, 128), F32),
            pltpu.VMEM((4 * comps, 128), F32),
            pltpu.VMEM((4 * comps, 128), F32),
            pltpu.VMEM((4 * comps, 128), F32),
            pltpu.SemaphoreType.DMA((4,)),
            pltpu.SemaphoreType.DMA((4,)),
            pltpu.SemaphoreType.DMA((4,)),
            pltpu.SemaphoreType.DMA((2,)),
            pltpu.SemaphoreType.DMA((2,)),
            pltpu.SemaphoreType.DMA((32,)),
            pltpu.SemaphoreType.DMA((32,)),
        ],
        compiler_params=pltpu.CompilerParams(
            collective_id=0, has_side_effects=True, vmem_limit_bytes=48 * 1024 * 1024
        ),
    )(
        samples.reshape(192, lon),
        legendre,
        cos_a,
        sin_a,
        cos_b,
        sin_b,
        spectral_state.reshape(512, comps),
        inv,
        live,
    )
    return out.reshape(64, 8, comps)


def solution(mesh):
    return jax.shard_map(
        functools.partial(body, mesh.shape["rad"]),
        mesh=mesh,
        in_specs=(
            P("rad", None, "lat", None),
            P("rad", "lat", None),
            P(),
            P(),
            P("lat", "rad", None),
            P("lat", None, None, None),
        ),
        out_specs=P("lat", "rad", None),
        check_vma=False,
    )
```

```python
import functools
import math

import jax
import jax.numpy as jnp
from jax import lax
from jax.experimental import pallas as pl
from jax.experimental.pallas import tpu as pltpu
from jax.sharding import PartitionSpec as P

MESH = pl.DeviceIdType.MESH
F32 = jnp.float32
BF16 = jnp.bfloat16
SEND_AT = (0, 1, 3, 5)


def cos_sin(waves, first, rows, order, period, scale):
    turns = lax.broadcasted_iota(jnp.int32, (rows, order.shape[1]), 0).astype(F32) * order
    phase = turns - period * jnp.floor((turns + 0.5) * (1.0 / period))
    quarter = jnp.floor(phase * (4.0 / period) + 0.5)
    rest = (phase - quarter * (period / 4.0)) * (2.0 * math.pi / period)
    q = rest * rest
    s = rest + rest * q * (-1 / 6 + q * (1 / 120 + q * (-1 / 5040 + q * (1 / 362880))))
    c = 1.0 + q * (-0.5 + q * (1 / 24 + q * (-1 / 720 + q * (1 / 40320 - q * (1 / 3628800)))))
    odd = (quarter == 1.0) | (quarter == 3.0)
    cos = jnp.where(odd, s, c)
    sin = jnp.where(odd, c, s)
    cos = jnp.where((quarter == 1.0) | (quarter == 2.0), -cos, cos)
    sin = jnp.where((quarter == 2.0) | (quarter == 3.0), -sin, sin)
    waves[0, first : first + rows, :] = cos * scale
    waves[1, first : first + rows, :] = sin * scale


def kernel(
    n_rad,
    samples_hbm,
    legendre,
    order_row,
    assign,
    counts,
    state_hbm,
    inverses_hbm,
    out,
    samples,
    state,
    inverses64,
    inverses,
    waves,
    table,
    send_rows,
    got_rows,
    rows32,
    modes,
    leg_own,
    leg_got,
    leg_mat,
    send_first,
    recv_first,
    send_buf,
    recv_buf,
    acc,
    fields,
    right,
    solved,
    in_sem,
    own_sem,
    zs_sem,
    zr_sem,
    as_sem,
    ar_sem,
    rs_sem,
    rr_sem,
):
    rad = lax.axis_index("rad")
    lat = lax.axis_index("lat")
    z = lat // 8
    y = lat % 8
    other = (1 - z) * 8 + y
    y_next = (z * 8 + (y + 1) % 8, z * 8 + (y + 7) % 8)
    n_r = n_rad
    kb = n_r // 4
    comps = 4 * n_r
    lon = samples.shape[1]
    lon_b = 32
    lon_a = lon // lon_b
    slots = order_row.shape[1]

    barrier = pltpu.get_barrier_semaphore()

    pl.semaphore_signal(barrier, inc=1, device_id=(rad, other), device_id_type=MESH)
    for d in range(2):
        pl.semaphore_signal(barrier, inc=1, device_id=(rad, y_next[d]), device_id_type=MESH)

    odd = y % 2
    way_a, way_b = 1 - odd, odd
    tile_of = [(y // 2 + o) % 4 for o in (2, 1 + 2 * odd, 3 + 2 * odd, 0)]

    def own_copy(c):
        lanes = pl.multiple_of(z * 512 + tile_of[c] * 128, 128)
        return pltpu.make_async_copy(
            legendre.at[:, :, pl.ds(lanes, 128)], leg_own.at[tile_of[c]], own_sem.at[c]
        )

    def z_copy(c):
        lanes = pl.multiple_of((1 - z) * 512 + tile_of[c] * 128, 128)
        return pltpu.make_async_remote_copy(
            src_ref=legendre.at[:, :, pl.ds(lanes, 128)],
            dst_ref=leg_got.at[tile_of[c]],
            send_sem=zs_sem.at[c],
            recv_sem=zr_sem.at[c],
            device_id=(rad, other),
            device_id_type=MESH,
        )

    inputs = [
        pltpu.make_async_copy(src, dst, in_sem.at[i])
        for i, (src, dst) in enumerate(
            ((samples_hbm, samples), (state_hbm, state), (inverses_hbm, inverses64))
        )
    ]
    for copy in inputs:
        copy.start()
    for c in range(4):
        own_copy(c).start()

    order = order_row[...].astype(F32)
    cos_sin(waves, 0, lon_a, order, lon_a, 1.0)
    cos_sin(waves, lon_a, lon_b, order, lon, 1.0 / math.sqrt(lon))

    def table_row(a):
        ca = waves[0, pl.ds(a, 1), :]
        sa = waves[1, pl.ds(a, 1), :]
        cb = waves[0, lon_a : lon_a + lon_b, :]
        sb = waves[1, lon_a : lon_a + lon_b, :]
        at = pl.multiple_of(a * lon_b, lon_b)
        table[pl.ds(at, lon_b), 0:slots] = (ca * cb - sa * sb).astype(BF16)
        table[pl.ds(at, lon_b), slots : 2 * slots] = (-(sa * cb + ca * sb)).astype(BF16)

    per = lon_a // n_rad

    @pl.loop(0, n_rad)
    def _(i):
        @pl.when(i > 0)
        def _():
            peer = (rad + i) % n_rad
            pl.semaphore_signal(barrier, inc=1, device_id=(peer, lat), device_id_type=MESH)
            pl.semaphore_signal(barrier, inc=1, device_id=(peer, other), device_id_type=MESH)

        for k in range(per):
            table_row(i * per + k)

    pl.semaphore_wait(barrier, 2 * (n_rad - 1) + 3)
    def z_start(place):
        for c in range(4):
            if SEND_AT[c] == place:
                z_copy(c).start()

    z_start(0)
    inputs[0].wait()
    fourier = jnp.dot(samples[...], table[...], preferred_element_type=F32)
    fourier = fourier.astype(BF16).astype(F32)
    wide = []
    for f in range(2):
        part = fourier[96 * f : 96 * (f + 1)]
        part = jnp.concatenate([part, jnp.zeros((32, 2 * slots), F32)], axis=0).T
        wide += [part[:slots], part[slots:]]
    free = lax.broadcasted_iota(jnp.int32, (slots, 128), 1) >= 96
    packed = [
        jnp.where(free, pltpu.roll(wide[3], 96 - 32 * c, 1), wide[c]).reshape(n_rad, 8, 128)
        for c in range(3)
    ]
    send_rows[...] = jnp.concatenate(packed, axis=1).astype(BF16)

    def a2a(peer, other_side):
        return pltpu.make_async_remote_copy(
            src_ref=send_rows.at[peer],
            dst_ref=got_rows.at[z, rad],
            send_sem=as_sem.at[other_side],
            recv_sem=ar_sem.at[other_side],
            device_id=(peer, other if other_side else lat),
            device_id_type=MESH,
        )

    a2a(rad, 1).start()

    @pl.loop(1, n_rad)
    def _(i):
        peer = (rad + i) % n_rad
        a2a(peer, 0).start()
        a2a(peer, 1).start()

    got_rows[z, rad] = send_rows[rad]
    z_start(1)

    leg_mat[:, :, :, 96:128, :] = jnp.zeros((2, 8, 4, 32, 128), BF16)
    leg_mat[:, :, :, 224:256, :] = jnp.zeros((2, 8, 4, 32, 128), BF16)
    low = lax.broadcasted_iota(jnp.int32, (96, 128), 1) < 64

    def lay(source, band, tile):
        @pl.loop(0, 4)
        def _(p):
            a = source[tile, 2 * p].astype(F32)
            b = source[tile, 2 * p + 1].astype(F32)
            ra = pltpu.roll(a, 64, 1)
            rb = pltpu.roll(b, 64, 1)
            zero = jnp.zeros_like(a)
            leg_mat[band, 2 * tile, p, 0:96, :] = jnp.where(low, a, zero).astype(BF16)
            leg_mat[band, 2 * tile, p, 128:224, :] = jnp.where(low, zero, rb).astype(BF16)
            leg_mat[band, 2 * tile + 1, p, 0:96, :] = jnp.where(low, ra, zero).astype(BF16)
            leg_mat[band, 2 * tile + 1, p, 128:224, :] = jnp.where(low, zero, b).astype(BF16)

    for c in range(4):
        own_copy(c).wait()
        lay(leg_own, 0, tile_of[c])

    inputs[1].wait()
    inputs[2].wait()
    inverses[...] = jnp.concatenate([inverses64[...], inverses64[...]], axis=1)
    for p in range(4):
        pair = jnp.concatenate(
            [state[pl.ds(2 * p, 64, stride=8), :], state[pl.ds(2 * p + 1, 64, stride=8), :]], axis=0
        )
        fields[comps * p : comps * (p + 1), :] = pair.T

    spacing = 0.65 / (n_r + 1)
    radius = [0.35 + 0.65 * (i + 1.0) / (n_r + 1) for i in range(n_r)]
    lane = lax.broadcasted_iota(jnp.int32, (1, 128), 1)
    left = lane < 64
    degree_id = lat * 64 + jnp.where(left, lane, lane - 64)
    degree = degree_id.astype(F32)
    live = []
    for p in range(4):
        lo, hi = assign[rad * 8 + 2 * p], assign[rad * 8 + 2 * p + 1]
        start = jnp.where(left, lo, hi)
        stop = jnp.where(left, lo + counts[lo], hi + counts[hi])
        live.append((degree_id >= start) & (degree_id < stop))
    square = 0.5 * spacing * spacing * degree * (degree + 1.0)
    for i in range(n_r):
        now = fields[pl.ds(i, 16, stride=n_r), :]
        value = -(square * (1.0 / (radius[i] * radius[i]))) * now
        ratio = spacing / radius[i]
        if i + 1 < n_r:
            value = value + (0.5 + 0.5 * ratio) * fields[pl.ds(i + 1, 16, stride=n_r), :]
        if i > 0:
            value = value + (0.5 - 0.5 * ratio) * fields[pl.ds(i - 1, 16, stride=n_r), :]
        right[pl.ds(i, 16, stride=n_r), :] = value

    lanes = lax.broadcasted_iota(jnp.int32, (n_r, 128), 1)

    def regroup(band, side):
        rows32[...] = got_rows[band].astype(F32).reshape(n_rad * 24, 128)
        for s in range(8):
            parts = [rows32[pl.ds(8 * c + s, n_r, stride=24), :] for c in range(3)]
            last = jnp.where(lanes < 32, pltpu.roll(parts[0], 32, 1), pltpu.roll(parts[1], 64, 1))
            last = jnp.where(lanes < 64, last, pltpu.roll(parts[2], 96, 1))
            for c, part in enumerate(parts + [last]):
                modes[side, s // 2, n_r * c : n_r * (c + 1), 128 * (s % 2) : 128 * (s % 2 + 1)] = (
                    part.astype(BF16)
                )

    def arrival(side, first):
        band = z if side == 0 else 1 - z
        return pltpu.make_async_remote_copy(
            src_ref=send_rows.at[pl.ds(first, n_rad - first)],
            dst_ref=got_rows.at[band, pl.ds(first, n_rad - first)],
            send_sem=as_sem.at[side],
            recv_sem=ar_sem.at[side],
            device_id=(rad, other),
            device_id_type=MESH,
        )

    arrival(0, 1).wait_recv()
    z_start(2)
    regroup(z, 0)
    arrival(1, 0).wait_recv()
    z_start(3)
    regroup(1 - z, 1)

    def own(d, p):
        total = None
        for side in range(2):
            band = jnp.dot(modes[side, p], leg_mat[side, d, p], preferred_element_type=F32)
            band = band.astype(BF16).astype(F32)
            total = band if total is None else total + band
        return total

    def hop(way, h, p, first):
        i = (way * 4 + h - 1) * 4 + p
        return pltpu.make_async_remote_copy(
            src_ref=send_first.at[way, p] if first else send_buf.at[way, h - 1, p],
            dst_ref=recv_first.at[way, p] if first else recv_buf.at[way, h - 1, p],
            send_sem=rs_sem.at[i],
            recv_sem=rr_sem.at[i],
            device_id=(rad, z * 8 + (y + 1 + 6 * way) % 8),
            device_id_type=MESH,
        )

    def steps(way, h, start):
        for i in range(2):
            p = 2 * way + i if start == 4 else 2 * (1 - way) + i
            total = own((y + h + way * (8 - 2 * h)) % 8, p)
            if h == start:
                send_first[way, p] = total.astype(BF16)
            else:
                hop(way, h + 1, p, h + 1 == start).wait_recv()
                if h + 1 == start:
                    total = total + recv_first[way, p].astype(F32)
                else:
                    total = total + recv_buf[way, h, p]
                send_buf[way, h - 1, p] = total
            hop(way, h, p, h == start).start()

    def block(c):
        z_copy(c).wait_recv()
        lay(leg_got, 1, tile_of[c])
        z_start(4 + c)

    block(0)
    steps(way_a, 4, 4)
    steps(way_b, 4, 4)
    steps(way_a, 3, 3)
    steps(way_a, 3, 4)
    block(1)
    steps(way_b, 3, 3)
    steps(way_b, 3, 4)
    steps(way_b, 2, 3)
    steps(way_b, 2, 4)
    block(2)
    steps(way_a, 2, 3)
    steps(way_a, 2, 4)
    steps(way_a, 1, 3)
    steps(way_a, 1, 4)
    block(3)
    steps(way_b, 1, 3)
    steps(way_b, 1, 4)

    for p in range(4):
        acc[comps * p : comps * (p + 1), :] = own(y, p)
    for p in range(4):
        total = acc[comps * p : comps * (p + 1), :]
        for way in range(2):
            hop(way, 1, p, False).wait_recv()
            total = total + recv_buf[way, 0, p]
        total = jnp.where(live[p], total, jnp.zeros_like(total))
        rows = slice(comps * p, comps * (p + 1))
        right[rows, :] = right[rows, :] + total

    ratios = [spacing / radius[i] for i in range(n_r)]
    lower = [-0.5 * (1.0 - ratios[k * kb]) for k in range(4)]
    upper = [-0.5 * (1.0 + ratios[(k + 1) * kb - 1]) for k in range(4)]
    carried = None
    forward = []
    for k in range(4):
        b = [right[pl.ds(k * kb + j, 16, stride=n_r), :] for j in range(kb)]
        if k > 0:
            b[0] = b[0] - lower[k] * carried
        rows = []
        for i in range(kb):
            value = None
            for j in range(kb):
                at = (k * kb + i) * kb + j
                term = inverses[at : at + 1, :] * b[j]
                value = term if value is None else value + term
            rows.append(value)
        forward.append(rows)
        carried = rows[kb - 1]
    carried = None
    for k in (3, 2, 1, 0):
        rows = forward[k]
        if k < 3:
            scaled = upper[k] * carried
            rows = [
                rows[i]
                - scaled * inverses[(k * kb + i) * kb + kb - 1 : (k * kb + i) * kb + kb, :]
                for i in range(kb)
            ]
        carried = rows[0]
        for i in range(kb):
            solved[pl.ds(k * kb + i, 16, stride=n_r), :] = rows[i]
    for p in range(4):
        flipped = solved[comps * p : comps * (p + 1), :].T
        out[pl.ds(2 * p, 64, stride=8), :] = flipped[:64]
        out[pl.ds(2 * p + 1, 64, stride=8), :] = flipped[64:]

    for c in range(4):
        z_copy(c).wait_send()
    arrival(0, 1).wait_send()
    arrival(1, 0).wait_send()
    for way in range(2):
        for p in range(4):
            start = 4 if p // 2 == way else 3
            for h in range(1, start + 1):
                hop(way, h, p, h == start).wait_send()


def body(n_rad, samples, legendre, assign, counts, spectral_state, inverses):
    lon = samples.shape[3]
    kb = inverses.shape[2]
    comps = 16 * kb
    slots = assign.shape[0]
    inv = jnp.transpose(inverses, (1, 2, 3, 0)).reshape(4 * kb * kb, 64)

    vmem = pl.BlockSpec(memory_space=pltpu.VMEM)
    smem = pl.BlockSpec(memory_space=pltpu.SMEM)
    hbm = pl.BlockSpec(memory_space=pltpu.HBM)
    out = pl.pallas_call(
        functools.partial(kernel, n_rad),
        out_shape=jax.ShapeDtypeStruct((512, comps), F32),
        in_specs=[hbm, hbm, vmem, smem, smem, hbm, hbm],
        out_specs=vmem,
        scratch_shapes=[
            pltpu.VMEM((192, lon), BF16),
            pltpu.VMEM((512, comps), F32),
            pltpu.VMEM((4 * kb * kb, 64), F32),
            pltpu.VMEM((4 * kb * kb, 128), F32),
            pltpu.VMEM((2, lon // 32 + 32, slots), F32),
            pltpu.VMEM((lon, 2 * slots), BF16),
            pltpu.VMEM((n_rad, 24, 128), BF16),
            pltpu.VMEM((2, n_rad, 24, 128), BF16),
            pltpu.VMEM((n_rad * 24, 128), F32),
            pltpu.VMEM((2, 4, comps, 256), BF16),
            pltpu.VMEM((4, 8, 96, 128), BF16),
            pltpu.VMEM((4, 8, 96, 128), BF16),
            pltpu.VMEM((2, 8, 4, 256, 128), BF16),
            pltpu.VMEM((2, 4, comps, 128), BF16),
            pltpu.VMEM((2, 4, comps, 128), BF16),
            pltpu.VMEM((2, 3, 4, comps, 128), F32),
            pltpu.VMEM((2, 3, 4, comps, 128), F32),
            pltpu.VMEM((4 * comps, 128), F32),
            pltpu.VMEM((4 * comps, 128), F32),
            pltpu.VMEM((4 * comps, 128), F32),
            pltpu.VMEM((4 * comps, 128), F32),
            pltpu.SemaphoreType.DMA((3,)),
            pltpu.SemaphoreType.DMA((4,)),
            pltpu.SemaphoreType.DMA((4,)),
            pltpu.SemaphoreType.DMA((4,)),
            pltpu.SemaphoreType.DMA((2,)),
            pltpu.SemaphoreType.DMA((2,)),
            pltpu.SemaphoreType.DMA((32,)),
            pltpu.SemaphoreType.DMA((32,)),
        ],
        compiler_params=pltpu.CompilerParams(
            collective_id=0, has_side_effects=True, vmem_limit_bytes=60 * 1024 * 1024
        ),
    )(
        samples.reshape(192, lon),
        legendre,
        assign.reshape(1, slots),
        assign,
        counts,
        spectral_state.reshape(512, comps),
        inv,
    )
    return out.reshape(64, 8, comps)


def solution(mesh):
    return jax.shard_map(
        functools.partial(body, mesh.shape["rad"]),
        mesh=mesh,
        in_specs=(
            P("rad", None, "lat", None),
            P("rad", "lat", None),
            P(),
            P(),
            P("lat", "rad", None),
            P("lat", None, None, None),
        ),
        out_specs=P("lat", "rad", None),
        check_vma=False,
    )
```

```python
import functools
import math

import jax
import jax.numpy as jnp
from jax import lax
from jax.experimental import pallas as pl
from jax.experimental.pallas import tpu as pltpu
from jax.sharding import PartitionSpec as P

MESH = pl.DeviceIdType.MESH
F32 = jnp.float32
BF16 = jnp.bfloat16
SEND_AT = (0, 1, 3, 5)
LONG = 1
WAIT_FIRST = True


def cos_sin(waves, first, rows, order, period, scale):
    turns = lax.broadcasted_iota(jnp.int32, (rows, order.shape[1]), 0).astype(F32) * order
    phase = turns - period * jnp.floor((turns + 0.5) * (1.0 / period))
    quarter = jnp.floor(phase * (4.0 / period) + 0.5)
    rest = (phase - quarter * (period / 4.0)) * (2.0 * math.pi / period)
    q = rest * rest
    s = rest + rest * q * (-1 / 6 + q * (1 / 120 + q * (-1 / 5040 + q * (1 / 362880))))
    c = 1.0 + q * (-0.5 + q * (1 / 24 + q * (-1 / 720 + q * (1 / 40320 - q * (1 / 3628800)))))
    odd = (quarter == 1.0) | (quarter == 3.0)
    cos = jnp.where(odd, s, c)
    sin = jnp.where(odd, c, s)
    cos = jnp.where((quarter == 1.0) | (quarter == 2.0), -cos, cos)
    sin = jnp.where((quarter == 2.0) | (quarter == 3.0), -sin, sin)
    waves[0, first : first + rows, :] = cos * scale
    waves[1, first : first + rows, :] = sin * scale


def kernel(
    n_rad,
    samples_hbm,
    legendre,
    order_row,
    assign,
    counts,
    state_hbm,
    inverses_hbm,
    out,
    samples,
    state,
    inverses64,
    inverses,
    waves,
    table,
    send_rows,
    got_rows,
    rows32,
    modes,
    leg_own,
    leg_got,
    leg_mat,
    send_half,
    recv_half,
    send_buf,
    recv_buf,
    acc,
    fields,
    right,
    solved,
    column_sem,
    in_sem,
    own_sem,
    zs_sem,
    zr_sem,
    as_sem,
    ar_sem,
    rs_sem,
    rr_sem,
):
    rad = lax.axis_index("rad")
    lat = lax.axis_index("lat")
    z = lat // 8
    y = lat % 8
    other = (1 - z) * 8 + y
    y_next = (z * 8 + (y + 1) % 8, z * 8 + (y + 7) % 8)
    n_r = n_rad
    kb = n_r // 4
    comps = 4 * n_r
    lon = samples.shape[1]
    lon_b = 32
    lon_a = lon // lon_b
    slots = order_row.shape[1]

    barrier = pltpu.get_barrier_semaphore()

    n_zh = n_rad // 8
    zh, xc = rad // 8, rad % 8

    def row_signal(semaphore):
        for i in range(1, 8):
            peer = zh * 8 + (xc + i) % 8
            pl.semaphore_signal(semaphore, inc=1, device_id=(peer, lat), device_id_type=MESH)

    pl.semaphore_signal(barrier, inc=1, device_id=(rad, other), device_id_type=MESH)
    for d in range(2):
        pl.semaphore_signal(barrier, inc=1, device_id=(rad, y_next[d]), device_id_type=MESH)
    for i in range(1, n_zh):
        peer = (zh + i) % n_zh * 8 + xc
        pl.semaphore_signal(barrier, inc=1, device_id=(peer, lat), device_id_type=MESH)
        pl.semaphore_signal(barrier, inc=1, device_id=(peer, other), device_id_type=MESH)
    row_signal(barrier)

    odd = y % 2
    way_a, way_b = 1 - odd, odd
    tile_of = [(y // 2 + o) % 4 for o in (2, 1 + 2 * odd, 3 + 2 * odd, 0)]

    def own_copy(c):
        lanes = pl.multiple_of(z * 512 + tile_of[c] * 128, 128)
        return pltpu.make_async_copy(
            legendre.at[:, :, pl.ds(lanes, 128)], leg_own.at[tile_of[c]], own_sem.at[c]
        )

    def z_copy(c):
        lanes = pl.multiple_of((1 - z) * 512 + tile_of[c] * 128, 128)
        return pltpu.make_async_remote_copy(
            src_ref=legendre.at[:, :, pl.ds(lanes, 128)],
            dst_ref=leg_got.at[tile_of[c]],
            send_sem=zs_sem.at[c],
            recv_sem=zr_sem.at[c],
            device_id=(rad, other),
            device_id_type=MESH,
        )

    inputs = [
        pltpu.make_async_copy(src, dst, in_sem.at[i])
        for i, (src, dst) in enumerate(
            ((samples_hbm, samples), (state_hbm, state), (inverses_hbm, inverses64))
        )
    ]
    for copy in inputs:
        copy.start()
    for c in range(4):
        own_copy(c).start()

    order = order_row[...].astype(F32)
    cos_sin(waves, 0, lon_a, order, lon_a, 1.0)
    cos_sin(waves, lon_a, lon_b, order, lon, 1.0 / math.sqrt(lon))

    def table_row(a):
        ca = waves[0, pl.ds(a, 1), :]
        sa = waves[1, pl.ds(a, 1), :]
        cb = waves[0, lon_a : lon_a + lon_b, :]
        sb = waves[1, lon_a : lon_a + lon_b, :]
        at = pl.multiple_of(a * lon_b, lon_b)
        table[pl.ds(at, lon_b), 0:slots] = (ca * cb - sa * sb).astype(BF16)
        table[pl.ds(at, lon_b), slots : 2 * slots] = (-(sa * cb + ca * sb)).astype(BF16)

    def z_start(place):
        for c in range(4):
            if SEND_AT[c] == place:
                z_copy(c).start()

    def greet():
        pl.semaphore_wait(barrier, 7 + 2 * n_zh - 1 + 2)
        z_start(0)
        row_signal(column_sem)

    if WAIT_FIRST:
        greet()
    per = 4

    @pl.loop(0, lon_a // per)
    def _(i):
        for k in range(per):
            table_row(i * per + k)

    if not WAIT_FIRST:
        greet()

    inputs[0].wait()
    fourier = jnp.dot(samples[...], table[...], preferred_element_type=F32)
    fourier = fourier.astype(BF16).astype(F32)
    wide = []
    for f in range(2):
        part = fourier[96 * f : 96 * (f + 1)]
        part = jnp.concatenate([part, jnp.zeros((32, 2 * slots), F32)], axis=0).T
        wide += [part[:slots], part[slots:]]
    free = lax.broadcasted_iota(jnp.int32, (slots, 128), 1) >= 96
    packed = [
        jnp.where(free, pltpu.roll(wide[3], 96 - 32 * c, 1), wide[c]).reshape(n_rad, 8, 128)
        for c in range(3)
    ]
    send_rows[...] = jnp.concatenate(packed, axis=1).astype(BF16)

    def a2a(peer, other_side):
        return pltpu.make_async_remote_copy(
            src_ref=send_rows.at[peer],
            dst_ref=got_rows.at[z, rad],
            send_sem=as_sem.at[other_side],
            recv_sem=ar_sem.at[other_side],
            device_id=(peer, other if other_side else lat),
            device_id_type=MESH,
        )

    pl.semaphore_wait(column_sem, 7)
    a2a(rad, 1).start()

    @pl.loop(1, n_rad)
    def _(i):
        peer = (rad + i) % n_rad
        a2a(peer, 0).start()
        a2a(peer, 1).start()

    got_rows[z, rad] = send_rows[rad]
    z_start(1)

    leg_mat[:, :, :, 96:128, :] = jnp.zeros((2, 8, 4, 32, 128), BF16)
    leg_mat[:, :, :, 224:256, :] = jnp.zeros((2, 8, 4, 32, 128), BF16)
    low = lax.broadcasted_iota(jnp.int32, (96, 128), 1) < 64

    def lay(source, band, tile):
        @pl.loop(0, 4)
        def _(p):
            a = source[tile, 2 * p].astype(F32)
            b = source[tile, 2 * p + 1].astype(F32)
            ra = pltpu.roll(a, 64, 1)
            rb = pltpu.roll(b, 64, 1)
            zero = jnp.zeros_like(a)
            leg_mat[band, 2 * tile, p, 0:96, :] = jnp.where(low, a, zero).astype(BF16)
            leg_mat[band, 2 * tile, p, 128:224, :] = jnp.where(low, zero, rb).astype(BF16)
            leg_mat[band, 2 * tile + 1, p, 0:96, :] = jnp.where(low, ra, zero).astype(BF16)
            leg_mat[band, 2 * tile + 1, p, 128:224, :] = jnp.where(low, zero, b).astype(BF16)

    for c in range(4):
        own_copy(c).wait()
        lay(leg_own, 0, tile_of[c])

    inputs[1].wait()
    inputs[2].wait()
    inverses[...] = jnp.concatenate([inverses64[...], inverses64[...]], axis=1)
    for p in range(4):
        pair = jnp.concatenate(
            [state[pl.ds(2 * p, 64, stride=8), :], state[pl.ds(2 * p + 1, 64, stride=8), :]], axis=0
        )
        fields[comps * p : comps * (p + 1), :] = pair.T

    spacing = 0.65 / (n_r + 1)
    radius = [0.35 + 0.65 * (i + 1.0) / (n_r + 1) for i in range(n_r)]
    lane = lax.broadcasted_iota(jnp.int32, (1, 128), 1)
    left = lane < 64
    degree_id = lat * 64 + jnp.where(left, lane, lane - 64)
    degree = degree_id.astype(F32)
    live = []
    for p in range(4):
        lo, hi = assign[rad * 8 + 2 * p], assign[rad * 8 + 2 * p + 1]
        start = jnp.where(left, lo, hi)
        stop = jnp.where(left, lo + counts[lo], hi + counts[hi])
        live.append((degree_id >= start) & (degree_id < stop))
    square = 0.5 * spacing * spacing * degree * (degree + 1.0)
    for i in range(n_r):
        now = fields[pl.ds(i, 16, stride=n_r), :]
        value = -(square * (1.0 / (radius[i] * radius[i]))) * now
        ratio = spacing / radius[i]
        if i + 1 < n_r:
            value = value + (0.5 + 0.5 * ratio) * fields[pl.ds(i + 1, 16, stride=n_r), :]
        if i > 0:
            value = value + (0.5 - 0.5 * ratio) * fields[pl.ds(i - 1, 16, stride=n_r), :]
        right[pl.ds(i, 16, stride=n_r), :] = value

    lanes = lax.broadcasted_iota(jnp.int32, (n_r, 128), 1)

    def regroup(band, side):
        rows32[...] = got_rows[band].astype(F32).reshape(n_rad * 24, 128)
        for s in range(8):
            parts = [rows32[pl.ds(8 * c + s, n_r, stride=24), :] for c in range(3)]
            last = jnp.where(lanes < 32, pltpu.roll(parts[0], 32, 1), pltpu.roll(parts[1], 64, 1))
            last = jnp.where(lanes < 64, last, pltpu.roll(parts[2], 96, 1))
            for c, part in enumerate(parts + [last]):
                modes[side, s // 2, n_r * c : n_r * (c + 1), 128 * (s % 2) : 128 * (s % 2 + 1)] = (
                    part.astype(BF16)
                )

    def arrival(side, first):
        band = z if side == 0 else 1 - z
        return pltpu.make_async_remote_copy(
            src_ref=send_rows.at[pl.ds(first, n_rad - first)],
            dst_ref=got_rows.at[band, pl.ds(first, n_rad - first)],
            send_sem=as_sem.at[side],
            recv_sem=ar_sem.at[side],
            device_id=(rad, other),
            device_id_type=MESH,
        )

    arrival(0, 1).wait_recv()
    z_start(2)
    regroup(z, 0)
    arrival(1, 0).wait_recv()
    z_start(3)
    regroup(1 - z, 1)

    def own(d, p):
        total = None
        for side in range(2):
            band = jnp.dot(modes[side, p], leg_mat[side, d, p], preferred_element_type=F32)
            band = band.astype(BF16).astype(F32)
            total = band if total is None else total + band
        return total

    def hop(way, h, p):
        i = (way * 4 + h - 1) * 4 + p
        return pltpu.make_async_remote_copy(
            src_ref=send_half.at[way, h - 1 - LONG, p] if h > LONG else send_buf.at[way, h - 1, p],
            dst_ref=recv_half.at[way, h - 1 - LONG, p] if h > LONG else recv_buf.at[way, h - 1, p],
            send_sem=rs_sem.at[i],
            recv_sem=rr_sem.at[i],
            device_id=(rad, z * 8 + (y + 1 + 6 * way) % 8),
            device_id_type=MESH,
        )

    def steps(way, h, start):
        for i in range(2):
            p = 2 * way + i if start == 4 else 2 * (1 - way) + i
            total = own((y + h + way * (8 - 2 * h)) % 8, p)
            if h < start:
                hop(way, h + 1, p).wait_recv()
                if h + 1 > LONG:
                    total = total + recv_half[way, h - LONG, p].astype(F32)
                else:
                    total = total + recv_buf[way, h, p]
            if h > LONG:
                send_half[way, h - 1 - LONG, p] = total.astype(BF16)
            else:
                send_buf[way, h - 1, p] = total
            hop(way, h, p).start()

    def block(c):
        z_copy(c).wait_recv()
        lay(leg_got, 1, tile_of[c])
        z_start(4 + c)

    block(0)
    steps(way_a, 4, 4)
    steps(way_b, 4, 4)
    steps(way_a, 3, 3)
    steps(way_a, 3, 4)
    block(1)
    steps(way_b, 3, 3)
    steps(way_b, 3, 4)
    steps(way_b, 2, 3)
    steps(way_b, 2, 4)
    block(2)
    steps(way_a, 2, 3)
    steps(way_a, 2, 4)
    steps(way_a, 1, 3)
    steps(way_a, 1, 4)
    block(3)
    steps(way_b, 1, 3)
    steps(way_b, 1, 4)

    for p in range(4):
        acc[comps * p : comps * (p + 1), :] = own(y, p)
    for p in range(4):
        total = acc[comps * p : comps * (p + 1), :]
        for way in range(2):
            hop(way, 1, p).wait_recv()
            total = total + recv_buf[way, 0, p]
        total = jnp.where(live[p], total, jnp.zeros_like(total))
        rows = slice(comps * p, comps * (p + 1))
        right[rows, :] = right[rows, :] + total

    ratios = [spacing / radius[i] for i in range(n_r)]
    lower = [-0.5 * (1.0 - ratios[k * kb]) for k in range(4)]
    upper = [-0.5 * (1.0 + ratios[(k + 1) * kb - 1]) for k in range(4)]
    carried = None
    forward = []
    for k in range(4):
        b = [right[pl.ds(k * kb + j, 16, stride=n_r), :] for j in range(kb)]
        if k > 0:
            b[0] = b[0] - lower[k] * carried
        rows = []
        for i in range(kb):
            value = None
            for j in range(kb):
                at = (k * kb + i) * kb + j
                term = inverses[at : at + 1, :] * b[j]
                value = term if value is None else value + term
            rows.append(value)
        forward.append(rows)
        carried = rows[kb - 1]
    carried = None
    for k in (3, 2, 1, 0):
        rows = forward[k]
        if k < 3:
            scaled = upper[k] * carried
            rows = [
                rows[i]
                - scaled * inverses[(k * kb + i) * kb + kb - 1 : (k * kb + i) * kb + kb, :]
                for i in range(kb)
            ]
        carried = rows[0]
        for i in range(kb):
            solved[pl.ds(k * kb + i, 16, stride=n_r), :] = rows[i]
    for p in range(4):
        flipped = solved[comps * p : comps * (p + 1), :].T
        out[pl.ds(2 * p, 64, stride=8), :] = flipped[:64]
        out[pl.ds(2 * p + 1, 64, stride=8), :] = flipped[64:]

    for c in range(4):
        z_copy(c).wait_send()
    arrival(0, 1).wait_send()
    arrival(1, 0).wait_send()
    for way in range(2):
        for p in range(4):
            start = 4 if p // 2 == way else 3
            for h in range(1, start + 1):
                hop(way, h, p).wait_send()


def body(n_rad, samples, legendre, assign, counts, spectral_state, inverses):
    lon = samples.shape[3]
    kb = inverses.shape[2]
    comps = 16 * kb
    slots = assign.shape[0]
    inv = jnp.transpose(inverses, (1, 2, 3, 0)).reshape(4 * kb * kb, 64)

    vmem = pl.BlockSpec(memory_space=pltpu.VMEM)
    smem = pl.BlockSpec(memory_space=pltpu.SMEM)
    hbm = pl.BlockSpec(memory_space=pltpu.HBM)
    out = pl.pallas_call(
        functools.partial(kernel, n_rad),
        out_shape=jax.ShapeDtypeStruct((512, comps), F32),
        in_specs=[hbm, hbm, vmem, smem, smem, hbm, hbm],
        out_specs=vmem,
        scratch_shapes=[
            pltpu.VMEM((192, lon), BF16),
            pltpu.VMEM((512, comps), F32),
            pltpu.VMEM((4 * kb * kb, 64), F32),
            pltpu.VMEM((4 * kb * kb, 128), F32),
            pltpu.VMEM((2, lon // 32 + 32, slots), F32),
            pltpu.VMEM((lon, 2 * slots), BF16),
            pltpu.VMEM((n_rad, 24, 128), BF16),
            pltpu.VMEM((2, n_rad, 24, 128), BF16),
            pltpu.VMEM((n_rad * 24, 128), F32),
            pltpu.VMEM((2, 4, comps, 256), BF16),
            pltpu.VMEM((4, 8, 96, 128), BF16),
            pltpu.VMEM((4, 8, 96, 128), BF16),
            pltpu.VMEM((2, 8, 4, 256, 128), BF16),
            pltpu.VMEM((2, 4 - LONG, 4, comps, 128), BF16),
            pltpu.VMEM((2, 4 - LONG, 4, comps, 128), BF16),
            pltpu.VMEM((2, LONG, 4, comps, 128), F32),
            pltpu.VMEM((2, LONG, 4, comps, 128), F32),
            pltpu.VMEM((4 * comps, 128), F32),
            pltpu.VMEM((4 * comps, 128), F32),
            pltpu.VMEM((4 * comps, 128), F32),
            pltpu.VMEM((4 * comps, 128), F32),
            pltpu.SemaphoreType.REGULAR,
            pltpu.SemaphoreType.DMA((3,)),
            pltpu.SemaphoreType.DMA((4,)),
            pltpu.SemaphoreType.DMA((4,)),
            pltpu.SemaphoreType.DMA((4,)),
            pltpu.SemaphoreType.DMA((2,)),
            pltpu.SemaphoreType.DMA((2,)),
            pltpu.SemaphoreType.DMA((32,)),
            pltpu.SemaphoreType.DMA((32,)),
        ],
        compiler_params=pltpu.CompilerParams(
            collective_id=0, has_side_effects=True, vmem_limit_bytes=60 * 1024 * 1024
        ),
    )(
        samples.reshape(192, lon),
        legendre,
        assign.reshape(1, slots),
        assign,
        counts,
        spectral_state.reshape(512, comps),
        inv,
    )
    return out.reshape(64, 8, comps)


def solution(mesh):
    return jax.shard_map(
        functools.partial(body, mesh.shape["rad"]),
        mesh=mesh,
        in_specs=(
            P("rad", None, "lat", None),
            P("rad", "lat", None),
            P(),
            P(),
            P("lat", "rad", None),
            P("lat", None, None, None),
        ),
        out_specs=P("lat", "rad", None),
        check_vma=False,
    )
```

```python
import functools
import math

import jax
import jax.numpy as jnp
from jax import lax
from jax.experimental import pallas as pl
from jax.experimental.pallas import tpu as pltpu
from jax.sharding import PartitionSpec as P

MESH = pl.DeviceIdType.MESH
F32 = jnp.float32
BF16 = jnp.bfloat16
SEND_AT = (0, 1, 3, 5)
WAIT_FIRST = True


def cos_sin(waves, first, rows, order, period, scale):
    turns = lax.broadcasted_iota(jnp.int32, (rows, order.shape[1]), 0).astype(F32) * order
    phase = turns - period * jnp.floor((turns + 0.5) * (1.0 / period))
    quarter = jnp.floor(phase * (4.0 / period) + 0.5)
    rest = (phase - quarter * (period / 4.0)) * (2.0 * math.pi / period)
    q = rest * rest
    s = rest + rest * q * (-1 / 6 + q * (1 / 120 + q * (-1 / 5040 + q * (1 / 362880))))
    c = 1.0 + q * (-0.5 + q * (1 / 24 + q * (-1 / 720 + q * (1 / 40320 - q * (1 / 3628800)))))
    odd = (quarter == 1.0) | (quarter == 3.0)
    cos = jnp.where(odd, s, c)
    sin = jnp.where(odd, c, s)
    cos = jnp.where((quarter == 1.0) | (quarter == 2.0), -cos, cos)
    sin = jnp.where((quarter == 2.0) | (quarter == 3.0), -sin, sin)
    waves[0, first : first + rows, :] = cos * scale
    waves[1, first : first + rows, :] = sin * scale


def kernel(
    n_rad,
    samples_hbm,
    legendre,
    order_row,
    assign,
    counts,
    state_hbm,
    inverses_hbm,
    out,
    samples,
    state,
    inverses64,
    inverses,
    waves,
    table,
    send_rows,
    got_rows,
    rows32,
    modes,
    leg_own,
    leg_got,
    leg_mat,
    send_buf,
    recv_buf,
    mine,
    fields,
    right,
    solved,
    column_sem,
    in_sem,
    own_sem,
    zs_sem,
    zr_sem,
    as_sem,
    ar_sem,
    rs_sem,
    rr_sem,
):
    rad = lax.axis_index("rad")
    lat = lax.axis_index("lat")
    z = lat // 8
    y = lat % 8
    other = (1 - z) * 8 + y
    y_next = (z * 8 + (y + 1) % 8, z * 8 + (y + 7) % 8)
    n_r = n_rad
    kb = n_r // 4
    comps = 4 * n_r
    lon = samples.shape[1]
    lon_b = 32
    lon_a = lon // lon_b
    slots = order_row.shape[1]

    barrier = pltpu.get_barrier_semaphore()

    n_zh = n_rad // 8
    zh, xc = rad // 8, rad % 8

    def row_signal(semaphore):
        for i in range(1, 8):
            peer = zh * 8 + (xc + i) % 8
            pl.semaphore_signal(semaphore, inc=1, device_id=(peer, lat), device_id_type=MESH)

    pl.semaphore_signal(barrier, inc=1, device_id=(rad, other), device_id_type=MESH)
    for d in range(2):
        pl.semaphore_signal(barrier, inc=1, device_id=(rad, y_next[d]), device_id_type=MESH)
    for i in range(1, n_zh):
        peer = (zh + i) % n_zh * 8 + xc
        pl.semaphore_signal(barrier, inc=1, device_id=(peer, lat), device_id_type=MESH)
        pl.semaphore_signal(barrier, inc=1, device_id=(peer, other), device_id_type=MESH)
    row_signal(barrier)

    odd = y % 2
    way_a, way_b = 1 - odd, odd
    tile_of = [(y // 2 + o) % 4 for o in (2, 1 + 2 * odd, 3 + 2 * odd, 0)]

    def own_copy(c):
        lanes = pl.multiple_of(z * 512 + tile_of[c] * 128, 128)
        return pltpu.make_async_copy(
            legendre.at[:, :, pl.ds(lanes, 128)], leg_own.at[tile_of[c]], own_sem.at[c]
        )

    def z_copy(c):
        lanes = pl.multiple_of((1 - z) * 512 + tile_of[c] * 128, 128)
        return pltpu.make_async_remote_copy(
            src_ref=legendre.at[:, :, pl.ds(lanes, 128)],
            dst_ref=leg_got.at[tile_of[c]],
            send_sem=zs_sem.at[c],
            recv_sem=zr_sem.at[c],
            device_id=(rad, other),
            device_id_type=MESH,
        )

    inputs = [
        pltpu.make_async_copy(src, dst, in_sem.at[i])
        for i, (src, dst) in enumerate(
            ((samples_hbm, samples), (state_hbm, state), (inverses_hbm, inverses64))
        )
    ]
    for copy in inputs:
        copy.start()
    for c in range(4):
        own_copy(c).start()

    order = order_row[...].astype(F32)
    cos_sin(waves, 0, lon_a, order, lon_a, 1.0)
    cos_sin(waves, lon_a, lon_b, order, lon, 1.0 / math.sqrt(lon))

    def table_row(a):
        ca = waves[0, pl.ds(a, 1), :]
        sa = waves[1, pl.ds(a, 1), :]
        cb = waves[0, lon_a : lon_a + lon_b, :]
        sb = waves[1, lon_a : lon_a + lon_b, :]
        at = pl.multiple_of(a * lon_b, lon_b)
        table[pl.ds(at, lon_b), 0:slots] = (ca * cb - sa * sb).astype(BF16)
        table[pl.ds(at, lon_b), slots : 2 * slots] = (-(sa * cb + ca * sb)).astype(BF16)

    def z_start(place):
        for c in range(4):
            if SEND_AT[c] == place:
                z_copy(c).start()

    def greet():
        pl.semaphore_wait(barrier, 7 + 2 * n_zh - 1 + 2)
        z_start(0)
        row_signal(column_sem)

    if WAIT_FIRST:
        greet()
    per = 4

    @pl.loop(0, lon_a // per)
    def _(i):
        for k in range(per):
            table_row(i * per + k)

    if not WAIT_FIRST:
        greet()

    inputs[0].wait()
    fourier = jnp.dot(samples[...], table[...], preferred_element_type=F32)
    fourier = fourier.astype(BF16).astype(F32)
    wide = []
    for f in range(2):
        part = fourier[96 * f : 96 * (f + 1)]
        part = jnp.concatenate([part, jnp.zeros((32, 2 * slots), F32)], axis=0).T
        wide += [part[:slots], part[slots:]]
    free = lax.broadcasted_iota(jnp.int32, (slots, 128), 1) >= 96
    packed = [
        jnp.where(free, pltpu.roll(wide[3], 96 - 32 * c, 1), wide[c]).reshape(n_rad, 8, 128)
        for c in range(3)
    ]
    send_rows[...] = jnp.concatenate(packed, axis=1).astype(BF16)

    def a2a(peer, other_side):
        return pltpu.make_async_remote_copy(
            src_ref=send_rows.at[peer],
            dst_ref=got_rows.at[z, rad],
            send_sem=as_sem.at[other_side],
            recv_sem=ar_sem.at[other_side],
            device_id=(peer, other if other_side else lat),
            device_id_type=MESH,
        )

    pl.semaphore_wait(column_sem, 7)

    @pl.loop(1, n_rad)
    def _(i):
        a2a((rad + i) % n_rad, 0).start()

    a2a(rad, 1).start()

    @pl.loop(1, n_rad)
    def _(i):
        a2a((rad + i) % n_rad, 1).start()


    got_rows[z, rad] = send_rows[rad]
    z_start(1)

    leg_mat[:, :, :, 96:128, :] = jnp.zeros((2, 4, 4, 32, 256), BF16)
    leg_mat[:, :, :, 224:256, :] = jnp.zeros((2, 4, 4, 32, 256), BF16)
    low = lax.broadcasted_iota(jnp.int32, (96, 128), 1) < 64

    def lay(source, band, tile):
        @pl.loop(0, 4)
        def _(p):
            a = source[tile, 2 * p].astype(F32)
            b = source[tile, 2 * p + 1].astype(F32)
            ra = pltpu.roll(a, 64, 1)
            rb = pltpu.roll(b, 64, 1)
            zero = jnp.zeros_like(a)
            leg_mat[band, tile, p, 0:96, 0:128] = jnp.where(low, a, zero).astype(BF16)
            leg_mat[band, tile, p, 128:224, 0:128] = jnp.where(low, zero, rb).astype(BF16)
            leg_mat[band, tile, p, 0:96, 128:256] = jnp.where(low, ra, zero).astype(BF16)
            leg_mat[band, tile, p, 128:224, 128:256] = jnp.where(low, zero, b).astype(BF16)

    for c in range(4):
        own_copy(c).wait()
        lay(leg_own, 0, tile_of[c])

    inputs[1].wait()
    inputs[2].wait()
    inverses[...] = jnp.concatenate([inverses64[...], inverses64[...]], axis=1)
    for p in range(4):
        pair = jnp.concatenate(
            [state[pl.ds(2 * p, 64, stride=8), :], state[pl.ds(2 * p + 1, 64, stride=8), :]], axis=0
        )
        fields[comps * p : comps * (p + 1), :] = pair.T

    spacing = 0.65 / (n_r + 1)
    radius = [0.35 + 0.65 * (i + 1.0) / (n_r + 1) for i in range(n_r)]
    lane = lax.broadcasted_iota(jnp.int32, (1, 128), 1)
    left = lane < 64
    degree_id = lat * 64 + jnp.where(left, lane, lane - 64)
    degree = degree_id.astype(F32)
    live = []
    for p in range(4):
        lo, hi = assign[rad * 8 + 2 * p], assign[rad * 8 + 2 * p + 1]
        start = jnp.where(left, lo, hi)
        stop = jnp.where(left, lo + counts[lo], hi + counts[hi])
        live.append((degree_id >= start) & (degree_id < stop))
    square = 0.5 * spacing * spacing * degree * (degree + 1.0)
    for i in range(n_r):
        now = fields[pl.ds(i, 16, stride=n_r), :]
        value = -(square * (1.0 / (radius[i] * radius[i]))) * now
        ratio = spacing / radius[i]
        if i + 1 < n_r:
            value = value + (0.5 + 0.5 * ratio) * fields[pl.ds(i + 1, 16, stride=n_r), :]
        if i > 0:
            value = value + (0.5 - 0.5 * ratio) * fields[pl.ds(i - 1, 16, stride=n_r), :]
        right[pl.ds(i, 16, stride=n_r), :] = value

    lanes = lax.broadcasted_iota(jnp.int32, (n_r, 128), 1)

    def regroup(band, side):
        rows32[...] = got_rows[band].astype(F32).reshape(n_rad * 24, 128)
        for s in range(8):
            parts = [rows32[pl.ds(8 * c + s, n_r, stride=24), :] for c in range(3)]
            last = jnp.where(lanes < 32, pltpu.roll(parts[0], 32, 1), pltpu.roll(parts[1], 64, 1))
            last = jnp.where(lanes < 64, last, pltpu.roll(parts[2], 96, 1))
            for c, part in enumerate(parts + [last]):
                modes[side, s // 2, n_r * c : n_r * (c + 1), 128 * (s % 2) : 128 * (s % 2 + 1)] = (
                    part.astype(BF16)
                )

    def arrival(side, first):
        band = z if side == 0 else 1 - z
        return pltpu.make_async_remote_copy(
            src_ref=send_rows.at[pl.ds(first, n_rad - first)],
            dst_ref=got_rows.at[band, pl.ds(first, n_rad - first)],
            send_sem=as_sem.at[side],
            recv_sem=ar_sem.at[side],
            device_id=(rad, other),
            device_id_type=MESH,
        )

    def share(side, tile):
        for p in range(4):
            band = jnp.dot(modes[side, p], leg_mat[side, tile, p], preferred_element_type=F32)
            band = band.astype(BF16).astype(F32)
            for k in range(2):
                part = band[:, 128 * k : 128 * (k + 1)]
                mine[2 * tile + k, p] = part if side == 0 else mine[2 * tile + k, p] + part

    def block(c):
        z_copy(c).wait_recv()
        lay(leg_got, 1, tile_of[c])
        z_start(4 + c)

    arrival(0, 1).wait_recv()
    z_start(2)
    regroup(z, 0)
    for c in range(4):
        share(0, tile_of[c])
    block(0)
    arrival(1, 0).wait_recv()
    z_start(3)
    regroup(1 - z, 1)
    share(1, tile_of[0])

    def hop(way, h, p):
        i = (way * 4 + h - 1) * 4 + p
        return pltpu.make_async_remote_copy(
            src_ref=send_buf.at[way, h - 1, p],
            dst_ref=recv_buf.at[way, h - 1, p],
            send_sem=rs_sem.at[i],
            recv_sem=rr_sem.at[i],
            device_id=(rad, z * 8 + (y + 1 + 6 * way) % 8),
            device_id_type=MESH,
        )

    def steps(way, h, start):
        for i in range(2):
            p = 2 * way + i if start == 4 else 2 * (1 - way) + i
            total = mine[(y + h + way * (8 - 2 * h)) % 8, p]
            if h < start:
                hop(way, h + 1, p).wait_recv()
                total = total + recv_buf[way, h, p].astype(F32)
            send_buf[way, h - 1, p] = total.astype(BF16)
            hop(way, h, p).start()

    steps(way_a, 4, 4)
    steps(way_b, 4, 4)
    steps(way_a, 3, 3)
    steps(way_a, 3, 4)
    block(1)
    share(1, tile_of[1])
    steps(way_b, 3, 3)
    steps(way_b, 3, 4)
    steps(way_b, 2, 3)
    steps(way_b, 2, 4)
    block(2)
    share(1, tile_of[2])
    steps(way_a, 2, 3)
    steps(way_a, 2, 4)
    steps(way_a, 1, 3)
    steps(way_a, 1, 4)
    block(3)
    share(1, tile_of[3])
    steps(way_b, 1, 3)
    steps(way_b, 1, 4)

    for p in range(4):
        total = mine[y, p]
        for way in range(2):
            hop(way, 1, p).wait_recv()
            total = total + recv_buf[way, 0, p].astype(F32)
        total = jnp.where(live[p], total, jnp.zeros_like(total))
        rows = slice(comps * p, comps * (p + 1))
        right[rows, :] = right[rows, :] + total

    ratios = [spacing / radius[i] for i in range(n_r)]
    lower = [-0.5 * (1.0 - ratios[k * kb]) for k in range(4)]
    upper = [-0.5 * (1.0 + ratios[(k + 1) * kb - 1]) for k in range(4)]
    carried = None
    forward = []
    for k in range(4):
        b = [right[pl.ds(k * kb + j, 16, stride=n_r), :] for j in range(kb)]
        if k > 0:
            b[0] = b[0] - lower[k] * carried
        rows = []
        for i in range(kb):
            value = None
            for j in range(kb):
                at = (k * kb + i) * kb + j
                term = inverses[at : at + 1, :] * b[j]
                value = term if value is None else value + term
            rows.append(value)
        forward.append(rows)
        carried = rows[kb - 1]
    carried = None
    for k in (3, 2, 1, 0):
        rows = forward[k]
        if k < 3:
            scaled = upper[k] * carried
            rows = [
                rows[i]
                - scaled * inverses[(k * kb + i) * kb + kb - 1 : (k * kb + i) * kb + kb, :]
                for i in range(kb)
            ]
        carried = rows[0]
        for i in range(kb):
            solved[pl.ds(k * kb + i, 16, stride=n_r), :] = rows[i]
    for p in range(4):
        flipped = solved[comps * p : comps * (p + 1), :].T
        out[pl.ds(2 * p, 64, stride=8), :] = flipped[:64]
        out[pl.ds(2 * p + 1, 64, stride=8), :] = flipped[64:]

    for c in range(4):
        z_copy(c).wait_send()
    arrival(0, 1).wait_send()
    arrival(1, 0).wait_send()
    for way in range(2):
        for p in range(4):
            start = 4 if p // 2 == way else 3
            for h in range(1, start + 1):
                hop(way, h, p).wait_send()


def body(n_rad, samples, legendre, assign, counts, spectral_state, inverses):
    lon = samples.shape[3]
    kb = inverses.shape[2]
    comps = 16 * kb
    slots = assign.shape[0]
    inv = jnp.transpose(inverses, (1, 2, 3, 0)).reshape(4 * kb * kb, 64)

    vmem = pl.BlockSpec(memory_space=pltpu.VMEM)
    smem = pl.BlockSpec(memory_space=pltpu.SMEM)
    hbm = pl.BlockSpec(memory_space=pltpu.HBM)
    out = pl.pallas_call(
        functools.partial(kernel, n_rad),
        out_shape=jax.ShapeDtypeStruct((512, comps), F32),
        in_specs=[hbm, hbm, vmem, smem, smem, hbm, hbm],
        out_specs=vmem,
        scratch_shapes=[
            pltpu.VMEM((192, lon), BF16),
            pltpu.VMEM((512, comps), F32),
            pltpu.VMEM((4 * kb * kb, 64), F32),
            pltpu.VMEM((4 * kb * kb, 128), F32),
            pltpu.VMEM((2, lon // 32 + 32, slots), F32),
            pltpu.VMEM((lon, 2 * slots), BF16),
            pltpu.VMEM((n_rad, 24, 128), BF16),
            pltpu.VMEM((2, n_rad, 24, 128), BF16),
            pltpu.VMEM((n_rad * 24, 128), F32),
            pltpu.VMEM((2, 4, comps, 256), BF16),
            pltpu.VMEM((4, 8, 96, 128), BF16),
            pltpu.VMEM((4, 8, 96, 128), BF16),
            pltpu.VMEM((2, 4, 4, 256, 256), BF16),
            pltpu.VMEM((2, 4, 4, comps, 128), BF16),
            pltpu.VMEM((2, 4, 4, comps, 128), BF16),
            pltpu.VMEM((8, 4, comps, 128), F32),
            pltpu.VMEM((4 * comps, 128), F32),
            pltpu.VMEM((4 * comps, 128), F32),
            pltpu.VMEM((4 * comps, 128), F32),
            pltpu.SemaphoreType.REGULAR,
            pltpu.SemaphoreType.DMA((3,)),
            pltpu.SemaphoreType.DMA((4,)),
            pltpu.SemaphoreType.DMA((4,)),
            pltpu.SemaphoreType.DMA((4,)),
            pltpu.SemaphoreType.DMA((2,)),
            pltpu.SemaphoreType.DMA((2,)),
            pltpu.SemaphoreType.DMA((32,)),
            pltpu.SemaphoreType.DMA((32,)),
        ],
        compiler_params=pltpu.CompilerParams(
            collective_id=0, has_side_effects=True, vmem_limit_bytes=60 * 1024 * 1024
        ),
    )(
        samples.reshape(192, lon),
        legendre,
        assign.reshape(1, slots),
        assign,
        counts,
        spectral_state.reshape(512, comps),
        inv,
    )
    return out.reshape(64, 8, comps)


def solution(mesh):
    return jax.shard_map(
        functools.partial(body, mesh.shape["rad"]),
        mesh=mesh,
        in_specs=(
            P("rad", None, "lat", None),
            P("rad", "lat", None),
            P(),
            P(),
            P("lat", "rad", None),
            P("lat", None, None, None),
        ),
        out_specs=P("lat", "rad", None),
        check_vma=False,
    )
```

```python
import functools
import math

import jax
import jax.numpy as jnp
from jax import lax
from jax.experimental import pallas as pl
from jax.experimental.pallas import tpu as pltpu
from jax.sharding import PartitionSpec as P

MESH = pl.DeviceIdType.MESH
F32 = jnp.float32
BF16 = jnp.bfloat16
SEND_AT = (0, 1, 3, 5)
WAIT_FIRST = True


def cos_sin(waves, first, rows, order, period, scale):
    turns = lax.broadcasted_iota(jnp.int32, (rows, order.shape[1]), 0).astype(F32) * order
    phase = turns - period * jnp.floor((turns + 0.5) * (1.0 / period))
    quarter = jnp.floor(phase * (4.0 / period) + 0.5)
    rest = (phase - quarter * (period / 4.0)) * (2.0 * math.pi / period)
    q = rest * rest
    s = rest + rest * q * (-1 / 6 + q * (1 / 120 + q * (-1 / 5040 + q * (1 / 362880))))
    c = 1.0 + q * (-0.5 + q * (1 / 24 + q * (-1 / 720 + q * (1 / 40320 - q * (1 / 3628800)))))
    odd = (quarter == 1.0) | (quarter == 3.0)
    cos = jnp.where(odd, s, c)
    sin = jnp.where(odd, c, s)
    cos = jnp.where((quarter == 1.0) | (quarter == 2.0), -cos, cos)
    sin = jnp.where((quarter == 2.0) | (quarter == 3.0), -sin, sin)
    waves[0, first : first + rows, :] = cos * scale
    waves[1, first : first + rows, :] = sin * scale


def kernel(
    n_rad,
    samples_hbm,
    legendre,
    order_row,
    assign,
    counts,
    state_hbm,
    inverses_hbm,
    out,
    samples,
    state,
    inverses64,
    inverses,
    waves,
    table,
    send_rows,
    got_rows,
    rows32,
    modes,
    leg_own,
    leg_got,
    leg_mat,
    send_buf,
    recv_buf,
    mine,
    fields,
    right,
    solved,
    column_sem,
    in_sem,
    own_sem,
    zs_sem,
    zr_sem,
    as_sem,
    ar_sem,
    rs_sem,
    rr_sem,
):
    rad = lax.axis_index("rad")
    lat = lax.axis_index("lat")
    z = lat // 8
    y = lat % 8
    other = (1 - z) * 8 + y
    y_next = (z * 8 + (y + 1) % 8, z * 8 + (y + 7) % 8)
    n_r = n_rad
    kb = n_r // 4
    comps = 4 * n_r
    lon = samples.shape[1]
    lon_b = 32
    lon_a = lon // lon_b
    slots = order_row.shape[1]

    barrier = pltpu.get_barrier_semaphore()

    n_zh = n_rad // 8
    zh, xc = rad // 8, rad % 8

    def row_signal(semaphore):
        for i in range(1, 8):
            peer = zh * 8 + (xc + i) % 8
            pl.semaphore_signal(semaphore, inc=1, device_id=(peer, lat), device_id_type=MESH)

    pl.semaphore_signal(barrier, inc=1, device_id=(rad, other), device_id_type=MESH)
    for d in range(2):
        pl.semaphore_signal(barrier, inc=1, device_id=(rad, y_next[d]), device_id_type=MESH)
    for i in range(1, n_zh):
        peer = (zh + i) % n_zh * 8 + xc
        pl.semaphore_signal(barrier, inc=1, device_id=(peer, lat), device_id_type=MESH)
        pl.semaphore_signal(barrier, inc=1, device_id=(peer, other), device_id_type=MESH)
    row_signal(barrier)

    odd = y % 2
    way_a, way_b = 1 - odd, odd
    tile_of = [(y // 2 + o) % 4 for o in (2, 1 + 2 * odd, 3 + 2 * odd, 0)]

    def own_copy(c):
        lanes = pl.multiple_of(z * 512 + tile_of[c] * 128, 128)
        return pltpu.make_async_copy(
            legendre.at[:, :, pl.ds(lanes, 128)], leg_own.at[tile_of[c]], own_sem.at[c]
        )

    def z_copy(c):
        lanes = pl.multiple_of((1 - z) * 512 + tile_of[c] * 128, 128)
        return pltpu.make_async_remote_copy(
            src_ref=legendre.at[:, :, pl.ds(lanes, 128)],
            dst_ref=leg_got.at[tile_of[c]],
            send_sem=zs_sem.at[c],
            recv_sem=zr_sem.at[c],
            device_id=(rad, other),
            device_id_type=MESH,
        )

    inputs = [
        pltpu.make_async_copy(src, dst, in_sem.at[i])
        for i, (src, dst) in enumerate(
            ((samples_hbm, samples), (state_hbm, state), (inverses_hbm, inverses64))
        )
    ]
    for copy in inputs:
        copy.start()
    for c in range(4):
        own_copy(c).start()

    order = order_row[...].astype(F32)
    cos_sin(waves, 0, lon_a, order, lon_a, 1.0)
    cos_sin(waves, lon_a, lon_b, order, lon, 1.0 / math.sqrt(lon))

    def table_row(a):
        ca = waves[0, pl.ds(a, 1), :]
        sa = waves[1, pl.ds(a, 1), :]
        cb = waves[0, lon_a : lon_a + lon_b, :]
        sb = waves[1, lon_a : lon_a + lon_b, :]
        at = pl.multiple_of(a * lon_b, lon_b)
        table[pl.ds(at, lon_b), 0:slots] = (ca * cb - sa * sb).astype(BF16)
        table[pl.ds(at, lon_b), slots : 2 * slots] = (-(sa * cb + ca * sb)).astype(BF16)

    def z_start(place):
        for c in range(4):
            if SEND_AT[c] == place:
                z_copy(c).start()

    def greet():
        pl.semaphore_wait(barrier, 7 + 2 * n_zh - 1 + 2)
        z_start(0)
        row_signal(column_sem)

    if WAIT_FIRST:
        greet()
    per = 4

    @pl.loop(0, lon_a // per)
    def _(i):
        for k in range(per):
            table_row(i * per + k)

    if not WAIT_FIRST:
        greet()

    inputs[0].wait()
    fourier = jnp.dot(samples[...], table[...], preferred_element_type=F32)
    fourier = fourier.astype(BF16).astype(F32)
    wide = []
    for f in range(2):
        part = fourier[96 * f : 96 * (f + 1)]
        part = jnp.concatenate([part, jnp.zeros((32, 2 * slots), F32)], axis=0).T
        wide += [part[:slots], part[slots:]]
    free = lax.broadcasted_iota(jnp.int32, (slots, 128), 1) >= 96
    packed = [
        jnp.where(free, pltpu.roll(wide[3], 96 - 32 * c, 1), wide[c]).reshape(n_rad, 8, 128)
        for c in range(3)
    ]
    send_rows[...] = jnp.concatenate(packed, axis=1).astype(BF16)

    def a2a(peer, other_side):
        return pltpu.make_async_remote_copy(
            src_ref=send_rows.at[peer],
            dst_ref=got_rows.at[z, rad],
            send_sem=as_sem.at[other_side],
            recv_sem=ar_sem.at[other_side],
            device_id=(peer, other if other_side else lat),
            device_id_type=MESH,
        )

    pl.semaphore_wait(column_sem, 7)

    @pl.loop(1, n_rad)
    def _(i):
        a2a((rad + (i + 14) % 31 + 1) % n_rad, 0).start()

    a2a(rad, 1).start()

    @pl.loop(1, n_rad)
    def _(i):
        a2a((rad + (i + 14) % 31 + 1) % n_rad, 1).start()


    got_rows[z, rad] = send_rows[rad]
    z_start(1)

    leg_mat[:, :, :, 96:128, :] = jnp.zeros((2, 4, 4, 32, 256), BF16)
    leg_mat[:, :, :, 224:256, :] = jnp.zeros((2, 4, 4, 32, 256), BF16)
    low = lax.broadcasted_iota(jnp.int32, (96, 128), 1) < 64

    def lay(source, band, tile):
        @pl.loop(0, 4)
        def _(p):
            a = source[tile, 2 * p].astype(F32)
            b = source[tile, 2 * p + 1].astype(F32)
            ra = pltpu.roll(a, 64, 1)
            rb = pltpu.roll(b, 64, 1)
            zero = jnp.zeros_like(a)
            leg_mat[band, tile, p, 0:96, 0:128] = jnp.where(low, a, zero).astype(BF16)
            leg_mat[band, tile, p, 128:224, 0:128] = jnp.where(low, zero, rb).astype(BF16)
            leg_mat[band, tile, p, 0:96, 128:256] = jnp.where(low, ra, zero).astype(BF16)
            leg_mat[band, tile, p, 128:224, 128:256] = jnp.where(low, zero, b).astype(BF16)

    for c in range(4):
        own_copy(c).wait()
        lay(leg_own, 0, tile_of[c])

    inputs[1].wait()
    inputs[2].wait()
    inverses[...] = jnp.concatenate([inverses64[...], inverses64[...]], axis=1)
    for p in range(4):
        pair = jnp.concatenate(
            [state[pl.ds(2 * p, 64, stride=8), :], state[pl.ds(2 * p + 1, 64, stride=8), :]], axis=0
        )
        fields[comps * p : comps * (p + 1), :] = pair.T

    spacing = 0.65 / (n_r + 1)
    radius = [0.35 + 0.65 * (i + 1.0) / (n_r + 1) for i in range(n_r)]
    lane = lax.broadcasted_iota(jnp.int32, (1, 128), 1)
    left = lane < 64
    degree_id = lat * 64 + jnp.where(left, lane, lane - 64)
    degree = degree_id.astype(F32)
    live = []
    for p in range(4):
        lo, hi = assign[rad * 8 + 2 * p], assign[rad * 8 + 2 * p + 1]
        start = jnp.where(left, lo, hi)
        stop = jnp.where(left, lo + counts[lo], hi + counts[hi])
        live.append((degree_id >= start) & (degree_id < stop))
    square = 0.5 * spacing * spacing * degree * (degree + 1.0)
    for i in range(n_r):
        now = fields[pl.ds(i, 16, stride=n_r), :]
        value = -(square * (1.0 / (radius[i] * radius[i]))) * now
        ratio = spacing / radius[i]
        if i + 1 < n_r:
            value = value + (0.5 + 0.5 * ratio) * fields[pl.ds(i + 1, 16, stride=n_r), :]
        if i > 0:
            value = value + (0.5 - 0.5 * ratio) * fields[pl.ds(i - 1, 16, stride=n_r), :]
        right[pl.ds(i, 16, stride=n_r), :] = value

    lanes = lax.broadcasted_iota(jnp.int32, (n_r, 128), 1)

    def regroup(band, side):
        rows32[...] = got_rows[band].astype(F32).reshape(n_rad * 24, 128)
        for s in range(8):
            parts = [rows32[pl.ds(8 * c + s, n_r, stride=24), :] for c in range(3)]
            last = jnp.where(lanes < 32, pltpu.roll(parts[0], 32, 1), pltpu.roll(parts[1], 64, 1))
            last = jnp.where(lanes < 64, last, pltpu.roll(parts[2], 96, 1))
            for c, part in enumerate(parts + [last]):
                modes[side, s // 2, n_r * c : n_r * (c + 1), 128 * (s % 2) : 128 * (s % 2 + 1)] = (
                    part.astype(BF16)
                )

    def arrival(side, first):
        band = z if side == 0 else 1 - z
        return pltpu.make_async_remote_copy(
            src_ref=send_rows.at[pl.ds(first, n_rad - first)],
            dst_ref=got_rows.at[band, pl.ds(first, n_rad - first)],
            send_sem=as_sem.at[side],
            recv_sem=ar_sem.at[side],
            device_id=(rad, other),
            device_id_type=MESH,
        )

    def share(side, tile):
        for p in range(4):
            band = jnp.dot(modes[side, p], leg_mat[side, tile, p], preferred_element_type=F32)
            band = band.astype(BF16).astype(F32)
            for k in range(2):
                part = band[:, 128 * k : 128 * (k + 1)]
                mine[2 * tile + k, p] = part if side == 0 else mine[2 * tile + k, p] + part

    def block(c):
        z_copy(c).wait_recv()
        lay(leg_got, 1, tile_of[c])
        z_start(4 + c)

    arrival(0, 1).wait_recv()
    z_start(2)
    regroup(z, 0)
    for c in range(4):
        share(0, tile_of[c])
    block(0)
    arrival(1, 0).wait_recv()
    z_start(3)
    regroup(1 - z, 1)
    share(1, tile_of[0])

    def hop(way, h, p):
        i = (way * 4 + h - 1) * 4 + p
        return pltpu.make_async_remote_copy(
            src_ref=send_buf.at[way, h - 1, p],
            dst_ref=recv_buf.at[way, h - 1, p],
            send_sem=rs_sem.at[i],
            recv_sem=rr_sem.at[i],
            device_id=(rad, z * 8 + (y + 1 + 6 * way) % 8),
            device_id_type=MESH,
        )

    def steps(way, h, start):
        for i in range(2):
            p = 2 * way + i if start == 4 else 2 * (1 - way) + i
            total = mine[(y + h + way * (8 - 2 * h)) % 8, p]
            if h < start:
                hop(way, h + 1, p).wait_recv()
                total = total + recv_buf[way, h, p].astype(F32)
            send_buf[way, h - 1, p] = total.astype(BF16)
            hop(way, h, p).start()

    steps(way_a, 4, 4)
    steps(way_b, 4, 4)
    steps(way_a, 3, 3)
    steps(way_a, 3, 4)
    block(1)
    share(1, tile_of[1])
    steps(way_b, 3, 3)
    steps(way_b, 3, 4)
    steps(way_b, 2, 3)
    steps(way_b, 2, 4)
    block(2)
    share(1, tile_of[2])
    steps(way_a, 2, 3)
    steps(way_a, 2, 4)
    steps(way_a, 1, 3)
    steps(way_a, 1, 4)
    block(3)
    share(1, tile_of[3])
    steps(way_b, 1, 3)
    steps(way_b, 1, 4)

    for p in range(4):
        total = mine[y, p]
        for way in range(2):
            hop(way, 1, p).wait_recv()
            total = total + recv_buf[way, 0, p].astype(F32)
        total = jnp.where(live[p], total, jnp.zeros_like(total))
        rows = slice(comps * p, comps * (p + 1))
        right[rows, :] = right[rows, :] + total

    ratios = [spacing / radius[i] for i in range(n_r)]
    lower = [-0.5 * (1.0 - ratios[k * kb]) for k in range(4)]
    upper = [-0.5 * (1.0 + ratios[(k + 1) * kb - 1]) for k in range(4)]
    carried = None
    forward = []
    for k in range(4):
        b = [right[pl.ds(k * kb + j, 16, stride=n_r), :] for j in range(kb)]
        if k > 0:
            b[0] = b[0] - lower[k] * carried
        rows = []
        for i in range(kb):
            value = None
            for j in range(kb):
                at = (k * kb + i) * kb + j
                term = inverses[at : at + 1, :] * b[j]
                value = term if value is None else value + term
            rows.append(value)
        forward.append(rows)
        carried = rows[kb - 1]
    carried = None
    for k in (3, 2, 1, 0):
        rows = forward[k]
        if k < 3:
            scaled = upper[k] * carried
            rows = [
                rows[i]
                - scaled * inverses[(k * kb + i) * kb + kb - 1 : (k * kb + i) * kb + kb, :]
                for i in range(kb)
            ]
        carried = rows[0]
        for i in range(kb):
            solved[pl.ds(k * kb + i, 16, stride=n_r), :] = rows[i]
    for p in range(4):
        flipped = solved[comps * p : comps * (p + 1), :].T
        out[pl.ds(2 * p, 64, stride=8), :] = flipped[:64]
        out[pl.ds(2 * p + 1, 64, stride=8), :] = flipped[64:]

    for c in range(4):
        z_copy(c).wait_send()
    arrival(0, 1).wait_send()
    arrival(1, 0).wait_send()
    for way in range(2):
        for p in range(4):
            start = 4 if p // 2 == way else 3
            for h in range(1, start + 1):
                hop(way, h, p).wait_send()


def body(n_rad, samples, legendre, assign, counts, spectral_state, inverses):
    lon = samples.shape[3]
    kb = inverses.shape[2]
    comps = 16 * kb
    slots = assign.shape[0]
    inv = jnp.transpose(inverses, (1, 2, 3, 0)).reshape(4 * kb * kb, 64)

    vmem = pl.BlockSpec(memory_space=pltpu.VMEM)
    smem = pl.BlockSpec(memory_space=pltpu.SMEM)
    hbm = pl.BlockSpec(memory_space=pltpu.HBM)
    out = pl.pallas_call(
        functools.partial(kernel, n_rad),
        out_shape=jax.ShapeDtypeStruct((512, comps), F32),
        in_specs=[hbm, hbm, vmem, smem, smem, hbm, hbm],
        out_specs=vmem,
        scratch_shapes=[
            pltpu.VMEM((192, lon), BF16),
            pltpu.VMEM((512, comps), F32),
            pltpu.VMEM((4 * kb * kb, 64), F32),
            pltpu.VMEM((4 * kb * kb, 128), F32),
            pltpu.VMEM((2, lon // 32 + 32, slots), F32),
            pltpu.VMEM((lon, 2 * slots), BF16),
            pltpu.VMEM((n_rad, 24, 128), BF16),
            pltpu.VMEM((2, n_rad, 24, 128), BF16),
            pltpu.VMEM((n_rad * 24, 128), F32),
            pltpu.VMEM((2, 4, comps, 256), BF16),
            pltpu.VMEM((4, 8, 96, 128), BF16),
            pltpu.VMEM((4, 8, 96, 128), BF16),
            pltpu.VMEM((2, 4, 4, 256, 256), BF16),
            pltpu.VMEM((2, 4, 4, comps, 128), BF16),
            pltpu.VMEM((2, 4, 4, comps, 128), BF16),
            pltpu.VMEM((8, 4, comps, 128), F32),
            pltpu.VMEM((4 * comps, 128), F32),
            pltpu.VMEM((4 * comps, 128), F32),
            pltpu.VMEM((4 * comps, 128), F32),
            pltpu.SemaphoreType.REGULAR,
            pltpu.SemaphoreType.DMA((3,)),
            pltpu.SemaphoreType.DMA((4,)),
            pltpu.SemaphoreType.DMA((4,)),
            pltpu.SemaphoreType.DMA((4,)),
            pltpu.SemaphoreType.DMA((2,)),
            pltpu.SemaphoreType.DMA((2,)),
            pltpu.SemaphoreType.DMA((32,)),
            pltpu.SemaphoreType.DMA((32,)),
        ],
        compiler_params=pltpu.CompilerParams(
            collective_id=0, has_side_effects=True, vmem_limit_bytes=60 * 1024 * 1024
        ),
    )(
        samples.reshape(192, lon),
        legendre,
        assign.reshape(1, slots),
        assign,
        counts,
        spectral_state.reshape(512, comps),
        inv,
    )
    return out.reshape(64, 8, comps)


def solution(mesh):
    return jax.shard_map(
        functools.partial(body, mesh.shape["rad"]),
        mesh=mesh,
        in_specs=(
            P("rad", None, "lat", None),
            P("rad", "lat", None),
            P(),
            P(),
            P("lat", "rad", None),
            P("lat", None, None, None),
        ),
        out_specs=P("lat", "rad", None),
        check_vma=False,
    )
```

```python
import functools
import math

import jax
import jax.numpy as jnp
from jax import lax
from jax.experimental import pallas as pl
from jax.experimental.pallas import tpu as pltpu
from jax.sharding import PartitionSpec as P

MESH = pl.DeviceIdType.MESH
F32 = jnp.float32
BF16 = jnp.bfloat16
SEND_AT = (0, 1, 3, 5, 5)
WAIT_FIRST = True


def cos_sin(waves, first, rows, order, period, scale):
    turns = lax.broadcasted_iota(jnp.int32, (rows, order.shape[1]), 0).astype(F32) * order
    phase = turns - period * jnp.floor((turns + 0.5) * (1.0 / period))
    quarter = jnp.floor(phase * (4.0 / period) + 0.5)
    rest = (phase - quarter * (period / 4.0)) * (2.0 * math.pi / period)
    q = rest * rest
    s = rest + rest * q * (-1 / 6 + q * (1 / 120 + q * (-1 / 5040 + q * (1 / 362880))))
    c = 1.0 + q * (-0.5 + q * (1 / 24 + q * (-1 / 720 + q * (1 / 40320 - q * (1 / 3628800)))))
    odd = (quarter == 1.0) | (quarter == 3.0)
    cos = jnp.where(odd, s, c)
    sin = jnp.where(odd, c, s)
    cos = jnp.where((quarter == 1.0) | (quarter == 2.0), -cos, cos)
    sin = jnp.where((quarter == 2.0) | (quarter == 3.0), -sin, sin)
    waves[0, first : first + rows, :] = cos * scale
    waves[1, first : first + rows, :] = sin * scale


def kernel(
    n_rad,
    samples_hbm,
    legendre,
    order_row,
    assign,
    counts,
    state_hbm,
    inverses_hbm,
    out,
    samples,
    state,
    inverses64,
    inverses,
    waves,
    table,
    send_rows,
    got_rows,
    rows32,
    modes,
    leg_own,
    leg_got,
    leg_mat,
    send_buf,
    recv_buf,
    mine,
    fields,
    right,
    solved,
    column_sem,
    in_sem,
    own_sem,
    zs_sem,
    zr_sem,
    as_sem,
    ar_sem,
    rs_sem,
    rr_sem,
):
    rad = lax.axis_index("rad")
    lat = lax.axis_index("lat")
    z = lat // 8
    y = lat % 8
    other = (1 - z) * 8 + y
    y_next = (z * 8 + (y + 1) % 8, z * 8 + (y + 7) % 8)
    n_r = n_rad
    kb = n_r // 4
    comps = 4 * n_r
    lon = samples.shape[1]
    lon_b = 32
    lon_a = lon // lon_b
    slots = order_row.shape[1]

    barrier = pltpu.get_barrier_semaphore()

    n_zh = n_rad // 8
    zh, xc = rad // 8, rad % 8

    def row_signal(semaphore):
        for i in range(1, 8):
            peer = zh * 8 + (xc + i) % 8
            pl.semaphore_signal(semaphore, inc=1, device_id=(peer, lat), device_id_type=MESH)

    pl.semaphore_signal(barrier, inc=1, device_id=(rad, other), device_id_type=MESH)
    for d in range(2):
        pl.semaphore_signal(barrier, inc=1, device_id=(rad, y_next[d]), device_id_type=MESH)
    for i in range(1, n_zh):
        peer = (zh + i) % n_zh * 8 + xc
        pl.semaphore_signal(barrier, inc=1, device_id=(peer, lat), device_id_type=MESH)
        pl.semaphore_signal(barrier, inc=1, device_id=(peer, other), device_id_type=MESH)
    row_signal(barrier)

    odd = y % 2
    way_a, way_b = 1 - odd, odd
    tile_of = [(y // 2 + o) % 4 for o in (2, 1 + 2 * odd, 3 + 2 * odd, 0)]

    def own_copy(c):
        lanes = pl.multiple_of(z * 512 + tile_of[c] * 128, 128)
        return pltpu.make_async_copy(
            legendre.at[:, :, pl.ds(lanes, 128)], leg_own.at[tile_of[c]], own_sem.at[c]
        )

    def z_copy(c):
        tile = tile_of[min(c, 3)]
        held = pl.ds(0, 8) if c < 3 else pl.ds(4 * (c - 3), 4)
        lanes = pl.multiple_of((1 - z) * 512 + tile * 128, 128)
        return pltpu.make_async_remote_copy(
            src_ref=legendre.at[held, :, pl.ds(lanes, 128)],
            dst_ref=leg_got.at[tile, held],
            send_sem=zs_sem.at[c],
            recv_sem=zr_sem.at[c],
            device_id=(rad, other),
            device_id_type=MESH,
        )

    inputs = [
        pltpu.make_async_copy(src, dst, in_sem.at[i])
        for i, (src, dst) in enumerate(
            ((samples_hbm, samples), (state_hbm, state), (inverses_hbm, inverses64))
        )
    ]
    for copy in inputs:
        copy.start()
    for c in range(4):
        own_copy(c).start()

    order = order_row[...].astype(F32)
    cos_sin(waves, 0, lon_a, order, lon_a, 1.0)
    cos_sin(waves, lon_a, lon_b, order, lon, 1.0 / math.sqrt(lon))

    def table_row(a):
        ca = waves[0, pl.ds(a, 1), :]
        sa = waves[1, pl.ds(a, 1), :]
        cb = waves[0, lon_a : lon_a + lon_b, :]
        sb = waves[1, lon_a : lon_a + lon_b, :]
        at = pl.multiple_of(a * lon_b, lon_b)
        table[pl.ds(at, lon_b), 0:slots] = (ca * cb - sa * sb).astype(BF16)
        table[pl.ds(at, lon_b), slots : 2 * slots] = (-(sa * cb + ca * sb)).astype(BF16)

    def z_start(place):
        for c in range(5):
            if SEND_AT[c] == place:
                z_copy(c).start()

    def greet():
        pl.semaphore_wait(barrier, 7 + 2 * n_zh - 1 + 2)
        z_start(0)
        row_signal(column_sem)

    if WAIT_FIRST:
        greet()
    per = 4

    @pl.loop(0, lon_a // per)
    def _(i):
        for k in range(per):
            table_row(i * per + k)

    if not WAIT_FIRST:
        greet()

    inputs[0].wait()
    fourier = jnp.dot(samples[...], table[...], preferred_element_type=F32)
    fourier = fourier.astype(BF16).astype(F32)
    wide = []
    for f in range(2):
        part = fourier[96 * f : 96 * (f + 1)]
        part = jnp.concatenate([part, jnp.zeros((32, 2 * slots), F32)], axis=0).T
        wide += [part[:slots], part[slots:]]
    free = lax.broadcasted_iota(jnp.int32, (slots, 128), 1) >= 96
    packed = [
        jnp.where(free, pltpu.roll(wide[3], 96 - 32 * c, 1), wide[c]).reshape(n_rad, 8, 128)
        for c in range(3)
    ]
    send_rows[...] = jnp.concatenate(packed, axis=1).astype(BF16)

    def a2a(peer, other_side):
        return pltpu.make_async_remote_copy(
            src_ref=send_rows.at[peer],
            dst_ref=got_rows.at[z, rad],
            send_sem=as_sem.at[other_side],
            recv_sem=ar_sem.at[other_side],
            device_id=(peer, other if other_side else lat),
            device_id_type=MESH,
        )

    pl.semaphore_wait(column_sem, 7)

    @pl.loop(1, n_rad)
    def _(i):
        a2a((rad + (i + 14) % 31 + 1) % n_rad, 0).start()

    a2a(rad, 1).start()

    @pl.loop(1, n_rad)
    def _(i):
        a2a((rad + (i + 14) % 31 + 1) % n_rad, 1).start()


    got_rows[z, rad] = send_rows[rad]
    z_start(1)

    leg_mat[:, :, :, 96:128, :] = jnp.zeros((2, 4, 4, 32, 256), BF16)
    leg_mat[:, :, :, 224:256, :] = jnp.zeros((2, 4, 4, 32, 256), BF16)
    low = lax.broadcasted_iota(jnp.int32, (96, 128), 1) < 64

    def lay(source, band, tile, first=0, end=4):
        @pl.loop(first, end)
        def _(p):
            a = source[tile, 2 * p].astype(F32)
            b = source[tile, 2 * p + 1].astype(F32)
            ra = pltpu.roll(a, 64, 1)
            rb = pltpu.roll(b, 64, 1)
            zero = jnp.zeros_like(a)
            leg_mat[band, tile, p, 0:96, 0:128] = jnp.where(low, a, zero).astype(BF16)
            leg_mat[band, tile, p, 128:224, 0:128] = jnp.where(low, zero, rb).astype(BF16)
            leg_mat[band, tile, p, 0:96, 128:256] = jnp.where(low, ra, zero).astype(BF16)
            leg_mat[band, tile, p, 128:224, 128:256] = jnp.where(low, zero, b).astype(BF16)

    for c in range(4):
        own_copy(c).wait()
        lay(leg_own, 0, tile_of[c])

    inputs[1].wait()
    inputs[2].wait()
    inverses[...] = jnp.concatenate([inverses64[...], inverses64[...]], axis=1)
    for p in range(4):
        pair = jnp.concatenate(
            [state[pl.ds(2 * p, 64, stride=8), :], state[pl.ds(2 * p + 1, 64, stride=8), :]], axis=0
        )
        fields[comps * p : comps * (p + 1), :] = pair.T

    spacing = 0.65 / (n_r + 1)
    radius = [0.35 + 0.65 * (i + 1.0) / (n_r + 1) for i in range(n_r)]
    lane = lax.broadcasted_iota(jnp.int32, (1, 128), 1)
    left = lane < 64
    degree_id = lat * 64 + jnp.where(left, lane, lane - 64)
    degree = degree_id.astype(F32)
    live = []
    for p in range(4):
        lo, hi = assign[rad * 8 + 2 * p], assign[rad * 8 + 2 * p + 1]
        start = jnp.where(left, lo, hi)
        stop = jnp.where(left, lo + counts[lo], hi + counts[hi])
        live.append((degree_id >= start) & (degree_id < stop))
    square = 0.5 * spacing * spacing * degree * (degree + 1.0)
    for i in range(n_r):
        now = fields[pl.ds(i, 16, stride=n_r), :]
        value = -(square * (1.0 / (radius[i] * radius[i]))) * now
        ratio = spacing / radius[i]
        if i + 1 < n_r:
            value = value + (0.5 + 0.5 * ratio) * fields[pl.ds(i + 1, 16, stride=n_r), :]
        if i > 0:
            value = value + (0.5 - 0.5 * ratio) * fields[pl.ds(i - 1, 16, stride=n_r), :]
        right[pl.ds(i, 16, stride=n_r), :] = value

    lanes = lax.broadcasted_iota(jnp.int32, (n_r, 128), 1)

    def regroup(band, side):
        rows32[...] = got_rows[band].astype(F32).reshape(n_rad * 24, 128)
        for s in range(8):
            parts = [rows32[pl.ds(8 * c + s, n_r, stride=24), :] for c in range(3)]
            last = jnp.where(lanes < 32, pltpu.roll(parts[0], 32, 1), pltpu.roll(parts[1], 64, 1))
            last = jnp.where(lanes < 64, last, pltpu.roll(parts[2], 96, 1))
            for c, part in enumerate(parts + [last]):
                modes[side, s // 2, n_r * c : n_r * (c + 1), 128 * (s % 2) : 128 * (s % 2 + 1)] = (
                    part.astype(BF16)
                )

    def arrival(side, first):
        band = z if side == 0 else 1 - z
        return pltpu.make_async_remote_copy(
            src_ref=send_rows.at[pl.ds(first, n_rad - first)],
            dst_ref=got_rows.at[band, pl.ds(first, n_rad - first)],
            send_sem=as_sem.at[side],
            recv_sem=ar_sem.at[side],
            device_id=(rad, other),
            device_id_type=MESH,
        )

    def share(side, tile, first=0, end=4):
        for p in range(first, end):
            band = jnp.dot(modes[side, p], leg_mat[side, tile, p], preferred_element_type=F32)
            band = band.astype(BF16).astype(F32)
            for k in range(2):
                part = band[:, 128 * k : 128 * (k + 1)]
                mine[2 * tile + k, p] = part if side == 0 else mine[2 * tile + k, p] + part

    def block(c):
        z_copy(c).wait_recv()
        pairs = (0, 4) if c < 3 else (2 * (c - 3), 2 * (c - 3) + 2)
        lay(leg_got, 1, tile_of[min(c, 3)], *pairs)
        z_start(4 + c)

    arrival(0, 1).wait_recv()
    z_start(2)
    regroup(z, 0)
    for c in range(4):
        share(0, tile_of[c])
    block(0)
    arrival(1, 0).wait_recv()
    z_start(3)
    regroup(1 - z, 1)
    share(1, tile_of[0])

    def hop(way, h, p):
        i = (way * 4 + h - 1) * 4 + p
        return pltpu.make_async_remote_copy(
            src_ref=send_buf.at[way, h - 1, p],
            dst_ref=recv_buf.at[way, h - 1, p],
            send_sem=rs_sem.at[i],
            recv_sem=rr_sem.at[i],
            device_id=(rad, z * 8 + (y + 1 + 6 * way) % 8),
            device_id_type=MESH,
        )

    def step(way, h, start, p):
        total = mine[(y + h + way * (8 - 2 * h)) % 8, p]
        if h < start:
            hop(way, h + 1, p).wait_recv()
            total = total + recv_buf[way, h, p].astype(F32)
        send_buf[way, h - 1, p] = total.astype(BF16)
        hop(way, h, p).start()

    def steps(way, h, start):
        for i in range(2):
            step(way, h, start, 2 * way + i if start == 4 else 2 * (1 - way) + i)

    steps(way_a, 4, 4)
    steps(way_b, 4, 4)
    steps(way_a, 3, 3)
    steps(way_a, 3, 4)
    block(1)
    share(1, tile_of[1])
    steps(way_b, 3, 3)
    steps(way_b, 3, 4)
    steps(way_b, 2, 3)
    steps(way_b, 2, 4)
    block(2)
    share(1, tile_of[2])
    steps(way_a, 2, 3)
    steps(way_a, 2, 4)
    steps(way_a, 1, 3)
    steps(way_a, 1, 4)
    for q in range(2):
        block(3 + q)
        share(1, tile_of[3], 2 * q, 2 * q + 2)
        for i in range(2):
            step(way_b, 1, 3, 2 * q + i)

    for p in range(4):
        total = mine[y, p]
        for way in range(2):
            hop(way, 1, p).wait_recv()
            total = total + recv_buf[way, 0, p].astype(F32)
        total = jnp.where(live[p], total, jnp.zeros_like(total))
        rows = slice(comps * p, comps * (p + 1))
        right[rows, :] = right[rows, :] + total

    ratios = [spacing / radius[i] for i in range(n_r)]
    lower = [-0.5 * (1.0 - ratios[k * kb]) for k in range(4)]
    upper = [-0.5 * (1.0 + ratios[(k + 1) * kb - 1]) for k in range(4)]
    carried = None
    forward = []
    for k in range(4):
        b = [right[pl.ds(k * kb + j, 16, stride=n_r), :] for j in range(kb)]
        if k > 0:
            b[0] = b[0] - lower[k] * carried
        rows = []
        for i in range(kb):
            value = None
            for j in range(kb):
                at = (k * kb + i) * kb + j
                term = inverses[at : at + 1, :] * b[j]
                value = term if value is None else value + term
            rows.append(value)
        forward.append(rows)
        carried = rows[kb - 1]
    carried = None
    for k in (3, 2, 1, 0):
        rows = forward[k]
        if k < 3:
            scaled = upper[k] * carried
            rows = [
                rows[i]
                - scaled * inverses[(k * kb + i) * kb + kb - 1 : (k * kb + i) * kb + kb, :]
                for i in range(kb)
            ]
        carried = rows[0]
        for i in range(kb):
            solved[pl.ds(k * kb + i, 16, stride=n_r), :] = rows[i]
    for p in range(4):
        flipped = solved[comps * p : comps * (p + 1), :].T
        out[pl.ds(2 * p, 64, stride=8), :] = flipped[:64]
        out[pl.ds(2 * p + 1, 64, stride=8), :] = flipped[64:]

    for c in range(5):
        z_copy(c).wait_send()
    arrival(0, 1).wait_send()
    arrival(1, 0).wait_send()
    for way in range(2):
        for p in range(4):
            start = 4 if p // 2 == way else 3
            for h in range(1, start + 1):
                hop(way, h, p).wait_send()


def body(n_rad, samples, legendre, assign, counts, spectral_state, inverses):
    lon = samples.shape[3]
    kb = inverses.shape[2]
    comps = 16 * kb
    slots = assign.shape[0]
    inv = jnp.transpose(inverses, (1, 2, 3, 0)).reshape(4 * kb * kb, 64)

    vmem = pl.BlockSpec(memory_space=pltpu.VMEM)
    smem = pl.BlockSpec(memory_space=pltpu.SMEM)
    hbm = pl.BlockSpec(memory_space=pltpu.HBM)
    out = pl.pallas_call(
        functools.partial(kernel, n_rad),
        out_shape=jax.ShapeDtypeStruct((512, comps), F32),
        in_specs=[hbm, hbm, vmem, smem, smem, hbm, hbm],
        out_specs=vmem,
        scratch_shapes=[
            pltpu.VMEM((192, lon), BF16),
            pltpu.VMEM((512, comps), F32),
            pltpu.VMEM((4 * kb * kb, 64), F32),
            pltpu.VMEM((4 * kb * kb, 128), F32),
            pltpu.VMEM((2, lon // 32 + 32, slots), F32),
            pltpu.VMEM((lon, 2 * slots), BF16),
            pltpu.VMEM((n_rad, 24, 128), BF16),
            pltpu.VMEM((2, n_rad, 24, 128), BF16),
            pltpu.VMEM((n_rad * 24, 128), F32),
            pltpu.VMEM((2, 4, comps, 256), BF16),
            pltpu.VMEM((4, 8, 96, 128), BF16),
            pltpu.VMEM((4, 8, 96, 128), BF16),
            pltpu.VMEM((2, 4, 4, 256, 256), BF16),
            pltpu.VMEM((2, 4, 4, comps, 128), BF16),
            pltpu.VMEM((2, 4, 4, comps, 128), BF16),
            pltpu.VMEM((8, 4, comps, 128), F32),
            pltpu.VMEM((4 * comps, 128), F32),
            pltpu.VMEM((4 * comps, 128), F32),
            pltpu.VMEM((4 * comps, 128), F32),
            pltpu.SemaphoreType.REGULAR,
            pltpu.SemaphoreType.DMA((3,)),
            pltpu.SemaphoreType.DMA((4,)),
            pltpu.SemaphoreType.DMA((5,)),
            pltpu.SemaphoreType.DMA((5,)),
            pltpu.SemaphoreType.DMA((2,)),
            pltpu.SemaphoreType.DMA((2,)),
            pltpu.SemaphoreType.DMA((32,)),
            pltpu.SemaphoreType.DMA((32,)),
        ],
        compiler_params=pltpu.CompilerParams(
            collective_id=0, has_side_effects=True, vmem_limit_bytes=60 * 1024 * 1024
        ),
    )(
        samples.reshape(192, lon),
        legendre,
        assign.reshape(1, slots),
        assign,
        counts,
        spectral_state.reshape(512, comps),
        inv,
    )
    return out.reshape(64, 8, comps)


def solution(mesh):
    return jax.shard_map(
        functools.partial(body, mesh.shape["rad"]),
        mesh=mesh,
        in_specs=(
            P("rad", None, "lat", None),
            P("rad", "lat", None),
            P(),
            P(),
            P("lat", "rad", None),
            P("lat", None, None, None),
        ),
        out_specs=P("lat", "rad", None),
        check_vma=False,
    )
```

```python
import functools
import math

import jax
import jax.numpy as jnp
from jax import lax
from jax.experimental import pallas as pl
from jax.experimental.pallas import tpu as pltpu
from jax.sharding import PartitionSpec as P

MESH = pl.DeviceIdType.MESH
F32 = jnp.float32
BF16 = jnp.bfloat16
SEND_AT = (0, 1, 3, 3, 5)
WAIT_FIRST = True


def cos_sin(waves, first, rows, order, period, scale):
    turns = lax.broadcasted_iota(jnp.int32, (rows, order.shape[1]), 0).astype(F32) * order
    phase = turns - period * jnp.floor((turns + 0.5) * (1.0 / period))
    quarter = jnp.floor(phase * (4.0 / period) + 0.5)
    rest = (phase - quarter * (period / 4.0)) * (2.0 * math.pi / period)
    q = rest * rest
    s = rest + rest * q * (-1 / 6 + q * (1 / 120 + q * (-1 / 5040 + q * (1 / 362880))))
    c = 1.0 + q * (-0.5 + q * (1 / 24 + q * (-1 / 720 + q * (1 / 40320 - q * (1 / 3628800)))))
    odd = (quarter == 1.0) | (quarter == 3.0)
    cos = jnp.where(odd, s, c)
    sin = jnp.where(odd, c, s)
    cos = jnp.where((quarter == 1.0) | (quarter == 2.0), -cos, cos)
    sin = jnp.where((quarter == 2.0) | (quarter == 3.0), -sin, sin)
    waves[0, first : first + rows, :] = cos * scale
    waves[1, first : first + rows, :] = sin * scale


def kernel(
    n_rad,
    samples_hbm,
    legendre,
    order_row,
    assign,
    counts,
    state_hbm,
    inverses_hbm,
    out,
    samples,
    state,
    inverses64,
    inverses,
    waves,
    table,
    send_rows,
    got_rows,
    rows32,
    modes,
    leg_own,
    leg_got,
    leg_mat,
    send_buf,
    recv_buf,
    mine,
    fields,
    right,
    solved,
    column_sem,
    in_sem,
    own_sem,
    zs_sem,
    zr_sem,
    as_sem,
    ar_sem,
    rs_sem,
    rr_sem,
):
    rad = lax.axis_index("rad")
    lat = lax.axis_index("lat")
    z = lat // 8
    y = lat % 8
    other = (1 - z) * 8 + y
    y_next = (z * 8 + (y + 1) % 8, z * 8 + (y + 7) % 8)
    n_r = n_rad
    kb = n_r // 4
    comps = 4 * n_r
    lon = samples.shape[1]
    lon_b = 32
    lon_a = lon // lon_b
    slots = order_row.shape[1]

    barrier = pltpu.get_barrier_semaphore()

    n_zh = n_rad // 8
    zh, xc = rad // 8, rad % 8

    def row_signal(semaphore):
        for i in range(1, 8):
            peer = zh * 8 + (xc + i) % 8
            pl.semaphore_signal(semaphore, inc=1, device_id=(peer, lat), device_id_type=MESH)

    pl.semaphore_signal(barrier, inc=1, device_id=(rad, other), device_id_type=MESH)
    for d in range(2):
        pl.semaphore_signal(barrier, inc=1, device_id=(rad, y_next[d]), device_id_type=MESH)
    for i in range(1, n_zh):
        peer = (zh + i) % n_zh * 8 + xc
        pl.semaphore_signal(barrier, inc=1, device_id=(peer, lat), device_id_type=MESH)
        pl.semaphore_signal(barrier, inc=1, device_id=(peer, other), device_id_type=MESH)
    row_signal(barrier)

    odd = y % 2
    way_a, way_b = 1 - odd, odd
    tile_of = [(y // 2 + o) % 4 for o in (2, 1 + 2 * odd, 3 + 2 * odd, 0)]

    def own_copy(c):
        lanes = pl.multiple_of(z * 512 + tile_of[c] * 128, 128)
        return pltpu.make_async_copy(
            legendre.at[:, :, pl.ds(lanes, 128)], leg_own.at[tile_of[c]], own_sem.at[c]
        )

    def z_copy(c):
        tile = tile_of[min(c, 3)]
        held = pl.ds(0, 8) if c < 3 else pl.ds(4 * (c - 3), 4)
        lanes = pl.multiple_of((1 - z) * 512 + tile * 128, 128)
        return pltpu.make_async_remote_copy(
            src_ref=legendre.at[held, :, pl.ds(lanes, 128)],
            dst_ref=leg_got.at[tile, held],
            send_sem=zs_sem.at[c],
            recv_sem=zr_sem.at[c],
            device_id=(rad, other),
            device_id_type=MESH,
        )

    inputs = [
        pltpu.make_async_copy(src, dst, in_sem.at[i])
        for i, (src, dst) in enumerate(
            ((samples_hbm, samples), (state_hbm, state), (inverses_hbm, inverses64))
        )
    ]
    for copy in inputs:
        copy.start()
    for c in range(4):
        own_copy(c).start()

    order = order_row[...].astype(F32)
    cos_sin(waves, 0, lon_a, order, lon_a, 1.0)
    cos_sin(waves, lon_a, lon_b, order, lon, 1.0 / math.sqrt(lon))

    def table_row(a):
        ca = waves[0, pl.ds(a, 1), :]
        sa = waves[1, pl.ds(a, 1), :]
        cb = waves[0, lon_a : lon_a + lon_b, :]
        sb = waves[1, lon_a : lon_a + lon_b, :]
        at = pl.multiple_of(a * lon_b, lon_b)
        table[pl.ds(at, lon_b), 0:slots] = (ca * cb - sa * sb).astype(BF16)
        table[pl.ds(at, lon_b), slots : 2 * slots] = (-(sa * cb + ca * sb)).astype(BF16)

    def z_start(place):
        for c in range(5):
            if SEND_AT[c] == place:
                z_copy(c).start()

    def greet():
        pl.semaphore_wait(barrier, 7 + 2 * n_zh - 1 + 2)
        z_start(0)
        row_signal(column_sem)

    if WAIT_FIRST:
        greet()
    per = 4

    @pl.loop(0, lon_a // per)
    def _(i):
        for k in range(per):
            table_row(i * per + k)

    if not WAIT_FIRST:
        greet()

    inputs[0].wait()
    fourier = jnp.dot(samples[...], table[...], preferred_element_type=F32)
    fourier = fourier.astype(BF16).astype(F32)
    wide = []
    for f in range(2):
        part = fourier[96 * f : 96 * (f + 1)]
        part = jnp.concatenate([part, jnp.zeros((32, 2 * slots), F32)], axis=0).T
        wide += [part[:slots], part[slots:]]
    free = lax.broadcasted_iota(jnp.int32, (slots, 128), 1) >= 96
    packed = [
        jnp.where(free, pltpu.roll(wide[3], 96 - 32 * c, 1), wide[c]).reshape(n_rad, 8, 128)
        for c in range(3)
    ]
    send_rows[...] = jnp.concatenate(packed, axis=1).astype(BF16)

    def a2a(peer, other_side):
        return pltpu.make_async_remote_copy(
            src_ref=send_rows.at[peer],
            dst_ref=got_rows.at[z, rad],
            send_sem=as_sem.at[other_side],
            recv_sem=ar_sem.at[other_side],
            device_id=(peer, other if other_side else lat),
            device_id_type=MESH,
        )

    pl.semaphore_wait(column_sem, 7)

    @pl.loop(1, n_rad)
    def _(i):
        a2a((rad + (i + 14) % 31 + 1) % n_rad, 0).start()

    a2a(rad, 1).start()

    @pl.loop(1, n_rad)
    def _(i):
        a2a((rad + (i + 14) % 31 + 1) % n_rad, 1).start()


    got_rows[z, rad] = send_rows[rad]
    z_start(1)

    leg_mat[:, :, :, 96:128, :] = jnp.zeros((2, 4, 4, 32, 256), BF16)
    leg_mat[:, :, :, 224:256, :] = jnp.zeros((2, 4, 4, 32, 256), BF16)
    low = lax.broadcasted_iota(jnp.int32, (96, 128), 1) < 64

    def lay(source, band, tile, first=0, end=4):
        @pl.loop(first, end)
        def _(p):
            a = source[tile, 2 * p].astype(F32)
            b = source[tile, 2 * p + 1].astype(F32)
            ra = pltpu.roll(a, 64, 1)
            rb = pltpu.roll(b, 64, 1)
            zero = jnp.zeros_like(a)
            leg_mat[band, tile, p, 0:96, 0:128] = jnp.where(low, a, zero).astype(BF16)
            leg_mat[band, tile, p, 128:224, 0:128] = jnp.where(low, zero, rb).astype(BF16)
            leg_mat[band, tile, p, 0:96, 128:256] = jnp.where(low, ra, zero).astype(BF16)
            leg_mat[band, tile, p, 128:224, 128:256] = jnp.where(low, zero, b).astype(BF16)

    for c in range(4):
        own_copy(c).wait()
        lay(leg_own, 0, tile_of[c])

    inputs[1].wait()
    inputs[2].wait()
    inverses[...] = jnp.concatenate([inverses64[...], inverses64[...]], axis=1)
    for p in range(4):
        pair = jnp.concatenate(
            [state[pl.ds(2 * p, 64, stride=8), :], state[pl.ds(2 * p + 1, 64, stride=8), :]], axis=0
        )
        fields[comps * p : comps * (p + 1), :] = pair.T

    spacing = 0.65 / (n_r + 1)
    radius = [0.35 + 0.65 * (i + 1.0) / (n_r + 1) for i in range(n_r)]
    lane = lax.broadcasted_iota(jnp.int32, (1, 128), 1)
    left = lane < 64
    degree_id = lat * 64 + jnp.where(left, lane, lane - 64)
    degree = degree_id.astype(F32)
    live = []
    for p in range(4):
        lo, hi = assign[rad * 8 + 2 * p], assign[rad * 8 + 2 * p + 1]
        start = jnp.where(left, lo, hi)
        stop = jnp.where(left, lo + counts[lo], hi + counts[hi])
        live.append((degree_id >= start) & (degree_id < stop))
    square = 0.5 * spacing * spacing * degree * (degree + 1.0)
    for i in range(n_r):
        now = fields[pl.ds(i, 16, stride=n_r), :]
        value = -(square * (1.0 / (radius[i] * radius[i]))) * now
        ratio = spacing / radius[i]
        if i + 1 < n_r:
            value = value + (0.5 + 0.5 * ratio) * fields[pl.ds(i + 1, 16, stride=n_r), :]
        if i > 0:
            value = value + (0.5 - 0.5 * ratio) * fields[pl.ds(i - 1, 16, stride=n_r), :]
        right[pl.ds(i, 16, stride=n_r), :] = value

    lanes = lax.broadcasted_iota(jnp.int32, (n_r, 128), 1)

    def regroup(band, side):
        rows32[...] = got_rows[band].astype(F32).reshape(n_rad * 24, 128)
        for s in range(8):
            parts = [rows32[pl.ds(8 * c + s, n_r, stride=24), :] for c in range(3)]
            last = jnp.where(lanes < 32, pltpu.roll(parts[0], 32, 1), pltpu.roll(parts[1], 64, 1))
            last = jnp.where(lanes < 64, last, pltpu.roll(parts[2], 96, 1))
            for c, part in enumerate(parts + [last]):
                modes[side, s // 2, n_r * c : n_r * (c + 1), 128 * (s % 2) : 128 * (s % 2 + 1)] = (
                    part.astype(BF16)
                )

    def arrival(side, first):
        band = z if side == 0 else 1 - z
        return pltpu.make_async_remote_copy(
            src_ref=send_rows.at[pl.ds(first, n_rad - first)],
            dst_ref=got_rows.at[band, pl.ds(first, n_rad - first)],
            send_sem=as_sem.at[side],
            recv_sem=ar_sem.at[side],
            device_id=(rad, other),
            device_id_type=MESH,
        )

    def share(side, tile, first=0, end=4):
        for p in range(first, end):
            band = jnp.dot(modes[side, p], leg_mat[side, tile, p], preferred_element_type=F32)
            band = band.astype(BF16).astype(F32)
            for k in range(2):
                part = band[:, 128 * k : 128 * (k + 1)]
                mine[2 * tile + k, p] = part if side == 0 else mine[2 * tile + k, p] + part

    def block(c):
        z_copy(c).wait_recv()
        pairs = (0, 4) if c < 3 else (2 * (c - 3), 2 * (c - 3) + 2)
        lay(leg_got, 1, tile_of[min(c, 3)], *pairs)
        z_start(4 + c)

    arrival(0, 1).wait_recv()
    z_start(2)
    regroup(z, 0)
    for c in range(4):
        share(0, tile_of[c])
    block(0)
    arrival(1, 0).wait_recv()
    z_start(3)
    regroup(1 - z, 1)
    share(1, tile_of[0])

    def hop(way, h, p):
        i = (way * 4 + h - 1) * 4 + p
        return pltpu.make_async_remote_copy(
            src_ref=send_buf.at[way, h - 1, p],
            dst_ref=recv_buf.at[way, h - 1, p],
            send_sem=rs_sem.at[i],
            recv_sem=rr_sem.at[i],
            device_id=(rad, z * 8 + (y + 1 + 6 * way) % 8),
            device_id_type=MESH,
        )

    def step(way, h, start, p):
        total = mine[(y + h + way * (8 - 2 * h)) % 8, p]
        if h < start:
            hop(way, h + 1, p).wait_recv()
            total = total + recv_buf[way, h, p].astype(F32)
        send_buf[way, h - 1, p] = total.astype(BF16)
        hop(way, h, p).start()

    def steps(way, h, start):
        for i in range(2):
            step(way, h, start, 2 * way + i if start == 4 else 2 * (1 - way) + i)

    steps(way_a, 4, 4)
    steps(way_b, 4, 4)
    steps(way_a, 3, 3)
    steps(way_a, 3, 4)
    block(1)
    share(1, tile_of[1])
    steps(way_b, 3, 3)
    steps(way_b, 3, 4)
    steps(way_b, 2, 3)
    steps(way_b, 2, 4)
    block(2)
    share(1, tile_of[2])
    steps(way_a, 2, 3)
    steps(way_a, 2, 4)
    steps(way_a, 1, 3)
    steps(way_a, 1, 4)
    for q in range(2):
        block(3 + q)
        share(1, tile_of[3], 2 * q, 2 * q + 2)
        for i in range(2):
            step(way_b, 1, 3, 2 * q + i)

    for p in range(4):
        total = mine[y, p]
        for way in range(2):
            hop(way, 1, p).wait_recv()
            total = total + recv_buf[way, 0, p].astype(F32)
        total = jnp.where(live[p], total, jnp.zeros_like(total))
        rows = slice(comps * p, comps * (p + 1))
        right[rows, :] = right[rows, :] + total

    ratios = [spacing / radius[i] for i in range(n_r)]
    lower = [-0.5 * (1.0 - ratios[k * kb]) for k in range(4)]
    upper = [-0.5 * (1.0 + ratios[(k + 1) * kb - 1]) for k in range(4)]
    carried = None
    forward = []
    for k in range(4):
        b = [right[pl.ds(k * kb + j, 16, stride=n_r), :] for j in range(kb)]
        if k > 0:
            b[0] = b[0] - lower[k] * carried
        rows = []
        for i in range(kb):
            value = None
            for j in range(kb):
                at = (k * kb + i) * kb + j
                term = inverses[at : at + 1, :] * b[j]
                value = term if value is None else value + term
            rows.append(value)
        forward.append(rows)
        carried = rows[kb - 1]
    carried = None
    for k in (3, 2, 1, 0):
        rows = forward[k]
        if k < 3:
            scaled = upper[k] * carried
            rows = [
                rows[i]
                - scaled * inverses[(k * kb + i) * kb + kb - 1 : (k * kb + i) * kb + kb, :]
                for i in range(kb)
            ]
        carried = rows[0]
        for i in range(kb):
            solved[pl.ds(k * kb + i, 16, stride=n_r), :] = rows[i]
    for p in range(4):
        flipped = solved[comps * p : comps * (p + 1), :].T
        out[pl.ds(2 * p, 64, stride=8), :] = flipped[:64]
        out[pl.ds(2 * p + 1, 64, stride=8), :] = flipped[64:]

    for c in range(5):
        z_copy(c).wait_send()
    arrival(0, 1).wait_send()
    arrival(1, 0).wait_send()
    for way in range(2):
        for p in range(4):
            start = 4 if p // 2 == way else 3
            for h in range(1, start + 1):
                hop(way, h, p).wait_send()


def body(n_rad, samples, legendre, assign, counts, spectral_state, inverses):
    lon = samples.shape[3]
    kb = inverses.shape[2]
    comps = 16 * kb
    slots = assign.shape[0]
    inv = jnp.transpose(inverses, (1, 2, 3, 0)).reshape(4 * kb * kb, 64)

    vmem = pl.BlockSpec(memory_space=pltpu.VMEM)
    smem = pl.BlockSpec(memory_space=pltpu.SMEM)
    hbm = pl.BlockSpec(memory_space=pltpu.HBM)
    out = pl.pallas_call(
        functools.partial(kernel, n_rad),
        out_shape=jax.ShapeDtypeStruct((512, comps), F32),
        in_specs=[hbm, hbm, vmem, smem, smem, hbm, hbm],
        out_specs=vmem,
        scratch_shapes=[
            pltpu.VMEM((192, lon), BF16),
            pltpu.VMEM((512, comps), F32),
            pltpu.VMEM((4 * kb * kb, 64), F32),
            pltpu.VMEM((4 * kb * kb, 128), F32),
            pltpu.VMEM((2, lon // 32 + 32, slots), F32),
            pltpu.VMEM((lon, 2 * slots), BF16),
            pltpu.VMEM((n_rad, 24, 128), BF16),
            pltpu.VMEM((2, n_rad, 24, 128), BF16),
            pltpu.VMEM((n_rad * 24, 128), F32),
            pltpu.VMEM((2, 4, comps, 256), BF16),
            pltpu.VMEM((4, 8, 96, 128), BF16),
            pltpu.VMEM((4, 8, 96, 128), BF16),
            pltpu.VMEM((2, 4, 4, 256, 256), BF16),
            pltpu.VMEM((2, 4, 4, comps, 128), BF16),
            pltpu.VMEM((2, 4, 4, comps, 128), BF16),
            pltpu.VMEM((8, 4, comps, 128), F32),
            pltpu.VMEM((4 * comps, 128), F32),
            pltpu.VMEM((4 * comps, 128), F32),
            pltpu.VMEM((4 * comps, 128), F32),
            pltpu.SemaphoreType.REGULAR,
            pltpu.SemaphoreType.DMA((3,)),
            pltpu.SemaphoreType.DMA((4,)),
            pltpu.SemaphoreType.DMA((5,)),
            pltpu.SemaphoreType.DMA((5,)),
            pltpu.SemaphoreType.DMA((2,)),
            pltpu.SemaphoreType.DMA((2,)),
            pltpu.SemaphoreType.DMA((32,)),
            pltpu.SemaphoreType.DMA((32,)),
        ],
        compiler_params=pltpu.CompilerParams(
            collective_id=0, has_side_effects=True, vmem_limit_bytes=60 * 1024 * 1024
        ),
    )(
        samples.reshape(192, lon),
        legendre,
        assign.reshape(1, slots),
        assign,
        counts,
        spectral_state.reshape(512, comps),
        inv,
    )
    return out.reshape(64, 8, comps)


def solution(mesh):
    return jax.shard_map(
        functools.partial(body, mesh.shape["rad"]),
        mesh=mesh,
        in_specs=(
            P("rad", None, "lat", None),
            P("rad", "lat", None),
            P(),
            P(),
            P("lat", "rad", None),
            P("lat", None, None, None),
        ),
        out_specs=P("lat", "rad", None),
        check_vma=False,
    )
```
